512 devices in a mesh: mode: 16 (over y, x), rest: 32 (over z, core).
Axes of the slice: x: 4, y: 4, z: 16, core: 2. Of those that a mesh axis runs over, the one named last changes fastest.
Arguments:
- unfolded: bfloat16 [1024, 131072], P('mode', 'rest'), as said below
- initial: float32 [1024, 128], P('mode'), may hold values from -6 to 6
Outputs:
- basis: float32 [1024, 128], P('mode')
- core: float32 [128, 131072], P('mode', 'rest')
The draws below stay inside these ranges and needn't reach their ends.
Inputs may be any that keep to these rules, and one draw needn't show every extreme that they name: `unfolded`: entries are bounded, with row and column scales that differ.
All inputs are finite; a program needn't handle non-finite values.
Results may differ from the reference program's by a relative error of at most 0.0029.
Values may be sent and summed in bfloat16 or wider, within the bound.
No kernel may reach another device: no remote copies, remote signals or barrier semaphores. Data moves between devices by JAX's collectives and lax.ppermute only.
A program may use at most 64 MiB of HBM per device.

```python
import jax
import jax.numpy as jnp
from jax import lax

I = 1024
RANK = 128
ITERS = 4
NCOL = 131072


def draw_unfolded(key, part):
    key = jax.random.fold_in(key, 1)
    first, second, third = jax.random.split(key, 3)
    row_scale = jnp.exp(jax.random.uniform(second, (I, 1), jnp.float32, jnp.log(0.4), jnp.log(4.0)))
    col_scale = jnp.exp(jax.random.uniform(third, (1, NCOL), jnp.float32, jnp.log(0.5), jnp.log(2.0)))
    values = jnp.clip(jax.random.normal(first, (I, NCOL), jnp.float32), -6.0, 6.0)
    return (values * row_scale * col_scale).astype(jnp.bfloat16)


def level_of(key, dims, cuts, low, high):
    def one(position, parts):
        steps = jax.random.uniform(jax.random.fold_in(jax.random.fold_in(key, 6), position), (parts,), jnp.float32, low / len(cuts), high / len(cuts))
        return jnp.repeat(jnp.exp(steps), dims[position] // parts).reshape((-1,) + (1,) * (len(dims) - position - 1))

    level = one(*cuts[0])
    for cut in cuts[1:]:
        level = level * one(*cut)
    return level


def bell_draw(stream_key, extent, width, bound, pieces=(), held_as=jnp.bfloat16):
    drawn = jax.random.normal(stream_key, extent, jnp.float32) * width
    if len(pieces) > 0:
        drawn = level_of(stream_key, extent, pieces, -0.22, 0.18) * drawn
    return jnp.clip(drawn, min=-bound, max=bound).astype(held_as)


def setup_inputs(seed: int = 0) -> dict:
    arg_keys = jax.random.split(jax.random.key(seed), 3)
    unfolded = draw_unfolded(jax.random.fold_in(arg_keys[2], 71), 0)
    initial = bell_draw(arg_keys[1], (I, RANK), 1.0, 6.0, ((0, 16),), jnp.float32)
    return {"unfolded": unfolded, "initial": initial}


def reference(unfolded, initial):
    gram = lax.dot_general(unfolded.astype(jnp.float32), unfolded.astype(jnp.float32), (((1,), (1,)), ((), ())), preferred_element_type=jnp.float32) / NCOL
    basis = initial
    for sweep in range(ITERS):
        image = jnp.dot(gram, basis, precision=lax.Precision.HIGHEST)
        correlation = jnp.dot(image.T, image, precision=lax.Precision.HIGHEST)
        factor = jnp.linalg.cholesky(correlation)
        basis = jax.scipy.linalg.solve_triangular(factor, image.T, lower=True).T
    basis_half = basis.astype(jnp.bfloat16)
    core = lax.dot_general(basis_half.astype(jnp.float32), unfolded.astype(jnp.float32), (((0,), (0,)), ((), ())), preferred_element_type=jnp.float32)
    return (basis, core)
```

```python
import jax
import jax.numpy as jnp
from jax import lax
from jax.experimental import pallas as pl
from jax.experimental.pallas import tpu as pltpu
from jax.sharding import Mesh, PartitionSpec as P

ITERS = 4
ROWS = 1024
RANK = 128
BLOCK = 128
HALF_BLOCKS = 18
SPLIT = 16
SLIVER = BLOCK // SPLIT
LEAST_PIVOT = 2e-3
MODE = ("y", "x")

SLOTS = [(t, t + d) for t in range(4) for d in range(4)]


def split_two(value):
    high = value.astype(jnp.bfloat16)
    return high, (value - high.astype(jnp.float32)).astype(jnp.bfloat16)


def dot_nt(left, right):
    return lax.dot_general(left, right, (((1,), (1,)), ((), ())), preferred_element_type=jnp.float32)


def dot_tn(left, right):
    return lax.dot_general(left, right, (((0,), (0,)), ((), ())), preferred_element_type=jnp.float32)


def dot_nn(left, right):
    return jnp.dot(left, right, preferred_element_type=jnp.float32)


def gram_kernel(place_ref, own_ref, twin_ref, out_ref):
    core = place_ref[0]

    def rows(ref, a):
        start = pl.multiple_of(lax.rem(core * 512 + a * 256, ROWS), 256)
        return ref[pl.ds(start, 256), :]

    own = [rows(own_ref, a) for a in range(4)]
    twin = [rows(twin_ref, a) for a in range(4)]
    tiles = {}
    for a, b in ((0, 0), (0, 1), (0, 2), (1, 1), (1, 2), (1, 3)):
        tiles[a, b] = dot_nt(own[a], own[b]) + dot_nt(twin[a], twin[b])

    def block(a, b):
        tile = tiles[a // 2, b // 2]
        return tile[(a % 2) * BLOCK : (a % 2 + 1) * BLOCK, (b % 2) * BLOCK : (b % 2 + 1) * BLOCK]

    for slot, (a, b) in enumerate(SLOTS):
        out_ref[:, slot] = block(a, b).reshape(SPLIT, SLIVER, BLOCK)
    for s in range(2):
        far = jnp.where(core == 0, block(s, s + 4), block(s + 2, s + 6))
        out_ref[:, 16 + s] = far.reshape(SPLIT, SLIVER, BLOCK)


def inverse_factor(corr, inv_ref):
    panels = RANK // 8
    row = lax.broadcasted_iota(jnp.int32, (8, RANK), 0)
    lane = lax.broadcasted_iota(jnp.int32, (8, RANK), 1)
    left = [corr[8 * p : 8 * p + 8, :] for p in range(panels)]
    right = [jnp.where(lane == row + 8 * p, 1.0, 0.0) for p in range(panels)]
    least = jnp.full((1, RANK), jnp.inf, jnp.float32)
    for p in range(panels):
        here, there = left[p], right[p]
        column = [jnp.broadcast_to(here[:, 8 * p + k : 8 * p + k + 1], (8, RANK)) for k in range(8)]
        scale = jnp.zeros((8, RANK), jnp.float32)
        for k in range(8):
            pivot = column[k][k : k + 1, :]
            root = lax.rsqrt(pivot)
            least = jnp.minimum(least, pivot)
            factor = jnp.where(row > k, column[k] * root, 0.0)
            for later in range(k + 1, 8):
                column[later] = column[later] - factor * (column[later][k : k + 1, :] * root)
            here = here - factor * (here[k : k + 1, :] * root)
            there = there - factor * (there[k : k + 1, :] * root)
            scale = jnp.where(row == k, root, scale)
        here, there = here * scale, there * scale
        inv_ref[8 * p : 8 * p + 8, :] = there
        turned = here.T
        for q in range(p + 1, panels):
            part = turned[8 * q : 8 * q + 8, :]
            for k in range(8):
                factor = jnp.broadcast_to(part[:, k : k + 1], (8, RANK))
                left[q] = left[q] - factor * here[k : k + 1, :]
                right[q] = right[q] - factor * there[k : k + 1, :]
    return jnp.min(least)


def iterate_kernel(columns, place_ref, own_ref, twin_ref, initial_ref, field_ref, basis_ref, core_ref,
                   high_ref, low_ref, pair_ref, image_ref, inv_ref):
    core, mode = place_ref[0], place_ref[1]
    scale = 1.0 / columns

    def put(a, b, value):
        def at(index):
            return pl.ds(pl.multiple_of(index * BLOCK, BLOCK), BLOCK) if not isinstance(index, int) else pl.ds(index * BLOCK, BLOCK)

        value = value.reshape(BLOCK, BLOCK) * scale
        high, low = split_two(value)
        high_ref[at(a), at(b)] = high
        low_ref[at(a), at(b)] = low
        if not (isinstance(a, int) and a == b):
            high, low = split_two(value.T)
            high_ref[at(b), at(a)] = high
            low_ref[at(b), at(a)] = low

    for slot, (a, b) in enumerate(SLOTS):
        put(a, b, own_ref[:, slot])
        put((a + 4) % 8, (b + 4) % 8, twin_ref[:, slot])
    for s in range(2):
        put(2 * core + s, 2 * core + s + 4, own_ref[:, 16 + s])
        put(6 - 2 * core + s, 2 - 2 * core + s, twin_ref[:, 16 + s])

    def set_pair(rows, value):
        high, low = split_two(value)
        pair_ref[rows, :RANK] = high
        pair_ref[rows, RANK:] = low

    def start():
        for half in range(2):
            offset = pl.multiple_of(lax.rem(core * 512 + half * 512, ROWS), 512)
            set_pair(pl.ds(half * 512, 512), initial_ref[pl.ds(offset, 512), :RANK])

    def multiply():
        pair = pair_ref[...]
        total = jnp.zeros((1, RANK), jnp.float32)
        for r in range(4):
            rows = pl.ds(r * 256, 256)
            both = dot_nn(high_ref[rows, :], pair)
            small = dot_nn(low_ref[rows, :], pair[:, :RANK])
            image = both[:, :RANK] + (both[:, RANK:] + small)
            image_ref[rows, :] = image
            total = total + jnp.sum(image * image, axis=0, keepdims=True)
        root = lax.rsqrt(total)
        for r in range(4):
            rows = pl.ds(r * 256, 256)
            set_pair(rows, image_ref[rows, :] * root)

    def orthonormalise():
        pair = pair_ref[...]
        corr = dot_tn(pair, pair)
        corr = (corr[:RANK, :RANK] + corr[RANK:, RANK:]) + (corr[:RANK, RANK:] + corr[RANK:, :RANK])
        least = inverse_factor(corr, inv_ref)
        high, low = split_two(inv_ref[...])
        weights = jnp.concatenate(
            [jnp.concatenate([high, high], axis=1), jnp.concatenate([low, jnp.zeros_like(low)], axis=1)], axis=0
        )
        for r in range(4):
            rows = pl.ds(r * 256, 256)
            both = dot_nt(pair[r * 256 : (r + 1) * 256], weights)
            value = both[:, :RANK] + both[:, RANK:]
            image_ref[rows, :] = value
            set_pair(rows, value)
        return least

    def step(carry):
        i, stop = carry
        pl.when(jnp.logical_or(i == 0, i == ITERS))(start)
        multiply()
        least = lax.cond(i >= ITERS - 1, orthonormalise, lambda: jnp.float32(1.0))
        sound = least >= LEAST_PIVOT
        stop = jnp.where(jnp.logical_and(i == ITERS - 1, jnp.logical_not(sound)), 2 * ITERS, stop)
        return i + 1, stop

    lax.while_loop(lambda carry: carry[0] < carry[1], step, (jnp.int32(0), jnp.int32(ITERS)))

    own_rows = ROWS // SPLIT
    basis_ref[...] = image_ref[pl.ds(pl.multiple_of(lax.rem(mode * own_rows + core * 512, ROWS), own_rows), own_rows), :]
    total = jnp.zeros((RANK, field_ref.shape[1]), jnp.float32)
    for half in range(2):
        offset = pl.multiple_of(lax.rem(core * 512 + half * 512, ROWS), 512)
        total = total + dot_tn(pair_ref[pl.ds(half * 512, 512), :RANK], field_ref[pl.ds(offset, 512), :])
    core_ref[...] = total.reshape(core_ref.shape)


def on_device(unfolded, initial):
    cols = unfolded.shape[1] // SPLIT
    columns = unfolded.shape[1] * lax.axis_size("z") * lax.axis_size("core")
    core, mode = lax.axis_index("core"), lax.axis_index(MODE)
    place = jnp.stack([core, mode]).astype(jnp.int32)
    vmem = pl.BlockSpec(memory_space=pltpu.VMEM)
    smem = pl.BlockSpec(memory_space=pltpu.SMEM)

    wide = jnp.concatenate([initial, initial, initial], axis=1)
    whole_initial = lax.all_gather(wide, MODE, axis=0, tiled=True)

    own = lax.all_to_all(unfolded, MODE, split_axis=1, concat_axis=0, tiled=True)
    twin = lax.ppermute(own, "core", [(0, 1), (1, 0)])
    partial_gram = pl.pallas_call(
        gram_kernel,
        out_shape=jax.ShapeDtypeStruct((SPLIT, HALF_BLOCKS, SLIVER, BLOCK), jnp.float32),
        in_specs=[smem, vmem, vmem],
        out_specs=vmem,
        name="gram",
    )(place, own, twin)
    got = lax.all_to_all(partial_gram, MODE, split_axis=0, concat_axis=0, tiled=True)
    sliver = jnp.sum(got, axis=0)
    deep = lax.axis_size("z")
    sliver = jnp.pad(sliver, ((0, 2 * deep - HALF_BLOCKS), (0, 0), (0, 0))).reshape(deep, 2, SLIVER, BLOCK)
    got = lax.all_to_all(sliver, "z", split_axis=0, concat_axis=0, tiled=True)
    got = jnp.broadcast_to(jnp.sum(got, axis=0)[None], got.shape)
    got = lax.all_to_all(got, "z", split_axis=0, concat_axis=0, tiled=True)
    got = got.reshape(2 * deep, SLIVER, BLOCK)[:HALF_BLOCKS]
    got = jnp.broadcast_to(got[None], (SPLIT,) + got.shape)
    own_gram = lax.all_to_all(got, MODE, split_axis=0, concat_axis=0, tiled=True)
    twin_gram = lax.ppermute(own_gram, "core", [(0, 1), (1, 0)])

    basis, core_rows = pl.pallas_call(
        lambda *refs: iterate_kernel(columns, *refs),
        out_shape=(
            jax.ShapeDtypeStruct((ROWS // SPLIT, RANK), jnp.float32),
            jax.ShapeDtypeStruct((SPLIT, RANK // SPLIT, cols), jnp.float32),
        ),
        in_specs=[smem, vmem, vmem, vmem, vmem],
        out_specs=(vmem, vmem),
        scratch_shapes=[
            pltpu.VMEM((ROWS, ROWS), jnp.bfloat16),
            pltpu.VMEM((ROWS, ROWS), jnp.bfloat16),
            pltpu.VMEM((ROWS, 2 * RANK), jnp.bfloat16),
            pltpu.VMEM((ROWS, RANK), jnp.float32),
            pltpu.VMEM((RANK, RANK), jnp.float32),
        ],
        compiler_params=pltpu.CompilerParams(vmem_limit_bytes=40 * 1024 * 1024),
        name="iterate",
    )(place, own_gram, twin_gram, whole_initial, own)
    core_cols = lax.all_to_all(core_rows, MODE, split_axis=0, concat_axis=0, tiled=True)
    return basis, core_cols.transpose(1, 0, 2).reshape(RANK // SPLIT, SPLIT * cols)


def solution(mesh):
    chips = Mesh(mesh.devices.reshape(4, 4, mesh.devices.shape[1] // 2, 2), ("y", "x", "z", "core"))
    in_specs = (P(MODE, ("z", "core")), P(MODE, None))
    out_specs = (P(MODE, None), P(MODE, ("z", "core")))
    return jax.shard_map(on_device, mesh=chips, in_specs=in_specs, out_specs=out_specs, check_vma=False)
```

```python
import jax
import jax.numpy as jnp
from jax import lax
from jax.experimental import pallas as pl
from jax.experimental.pallas import tpu as pltpu
from jax.sharding import Mesh, PartitionSpec as P

ITERS = 4
ROWS = 1024
RANK = 128
BLOCK = 128
HALF_BLOCKS = 18
SPLIT = 16
SLIVER = BLOCK // SPLIT
LEAST_PIVOT = 2e-3
MODE = ("y", "x")

SLOTS = [(t, t + d) for t in range(4) for d in range(4)]


def split_two(value):
    high = value.astype(jnp.bfloat16)
    return high, (value - high.astype(jnp.float32)).astype(jnp.bfloat16)


def dot_nt(left, right):
    return lax.dot_general(left, right, (((1,), (1,)), ((), ())), preferred_element_type=jnp.float32)


def dot_tn(left, right):
    return lax.dot_general(left, right, (((0,), (0,)), ((), ())), preferred_element_type=jnp.float32)


def dot_nn(left, right):
    return jnp.dot(left, right, preferred_element_type=jnp.float32)


def gram_kernel(place_ref, own_ref, twin_ref, out_ref):
    core = place_ref[0]
    cols = own_ref.shape[1] - RANK

    def rows(ref, a):
        start = pl.multiple_of(lax.rem(core * 512 + a * 256, ROWS), 256)
        return ref[pl.ds(start, 256), :cols]

    own = [rows(own_ref, a) for a in range(4)]
    twin = [rows(twin_ref, a) for a in range(4)]
    tiles = {}
    for a, b in ((0, 0), (0, 1), (0, 2), (1, 1), (1, 2), (1, 3)):
        tiles[a, b] = dot_nt(own[a], own[b]) + dot_nt(twin[a], twin[b])

    def block(a, b):
        tile = tiles[a // 2, b // 2]
        return tile[(a % 2) * BLOCK : (a % 2 + 1) * BLOCK, (b % 2) * BLOCK : (b % 2 + 1) * BLOCK]

    for slot, (a, b) in enumerate(SLOTS):
        out_ref[:, slot] = block(a, b).reshape(SPLIT, SLIVER, BLOCK)
    for s in range(2):
        far = jnp.where(core == 0, block(s, s + 4), block(s + 2, s + 6))
        out_ref[:, 16 + s] = far.reshape(SPLIT, SLIVER, BLOCK)


def inverse_factor(corr, inv_ref):
    panels = RANK // 8
    row = lax.broadcasted_iota(jnp.int32, (8, RANK), 0)
    lane = lax.broadcasted_iota(jnp.int32, (8, RANK), 1)
    left = [corr[8 * p : 8 * p + 8, :] for p in range(panels)]
    right = [jnp.where(lane == row + 8 * p, 1.0, 0.0) for p in range(panels)]
    least = jnp.full((1, RANK), jnp.inf, jnp.float32)
    for p in range(panels):
        here, there = left[p], right[p]
        column = [jnp.broadcast_to(here[:, 8 * p + k : 8 * p + k + 1], (8, RANK)) for k in range(8)]
        scale = jnp.zeros((8, RANK), jnp.float32)
        for k in range(8):
            pivot = column[k][k : k + 1, :]
            root = lax.rsqrt(pivot)
            least = jnp.minimum(least, pivot)
            factor = jnp.where(row > k, column[k] * root, 0.0)
            for later in range(k + 1, 8):
                column[later] = column[later] - factor * (column[later][k : k + 1, :] * root)
            here = here - factor * (here[k : k + 1, :] * root)
            there = there - factor * (there[k : k + 1, :] * root)
            scale = jnp.where(row == k, root, scale)
        here, there = here * scale, there * scale
        inv_ref[8 * p : 8 * p + 8, :] = there
        turned = here.T
        for q in range(p + 1, panels):
            part = turned[8 * q : 8 * q + 8, :]
            for k in range(8):
                factor = jnp.broadcast_to(part[:, k : k + 1], (8, RANK))
                left[q] = left[q] - factor * here[k : k + 1, :]
                right[q] = right[q] - factor * there[k : k + 1, :]
    return jnp.min(least)


def iterate_kernel(columns, cols, place_ref, own_ref, twin_ref, field_ref, twin_field_ref, basis_ref, core_ref,
                   high_ref, low_ref, pair_ref, image_ref, inv_ref):
    core, mode = place_ref[0], place_ref[1]
    scale = 1.0 / columns

    def put(a, b, value):
        def at(index):
            return pl.ds(pl.multiple_of(index * BLOCK, BLOCK), BLOCK) if not isinstance(index, int) else pl.ds(index * BLOCK, BLOCK)

        value = value.reshape(BLOCK, BLOCK) * scale
        high, low = split_two(value)
        high_ref[at(a), at(b)] = high
        low_ref[at(a), at(b)] = low
        if not (isinstance(a, int) and a == b):
            high, low = split_two(value.T)
            high_ref[at(b), at(a)] = high
            low_ref[at(b), at(a)] = low

    for slot, (a, b) in enumerate(SLOTS):
        put(a, b, own_ref[:, slot])
        put((a + 4) % 8, (b + 4) % 8, twin_ref[:, slot])
    for s in range(2):
        put(2 * core + s, 2 * core + s + 4, own_ref[:, 16 + s])
        put(6 - 2 * core + s, 2 - 2 * core + s, twin_ref[:, 16 + s])

    def set_pair(rows, value):
        high, low = split_two(value)
        pair_ref[rows, :RANK] = high
        pair_ref[rows, RANK:] = low

    def start():
        for half in range(2):
            offset = pl.multiple_of(lax.rem(core * 512 + half * 512, ROWS), 512)
            first = field_ref[pl.ds(offset, 512), cols:]
            second = twin_field_ref[pl.ds(offset, 512), cols:]
            pair_ref[pl.ds(half * 512, 512), :RANK] = jnp.where(core == 0, first, second)
            pair_ref[pl.ds(half * 512, 512), RANK:] = jnp.where(core == 0, second, first)

    def multiply():
        pair = pair_ref[...]
        total = jnp.zeros((1, RANK), jnp.float32)
        for r in range(4):
            rows = pl.ds(r * 256, 256)
            both = dot_nn(high_ref[rows, :], pair)
            small = dot_nn(low_ref[rows, :], pair[:, :RANK])
            image = both[:, :RANK] + (both[:, RANK:] + small)
            image_ref[rows, :] = image
            total = total + jnp.sum(image * image, axis=0, keepdims=True)
        root = lax.rsqrt(total)
        for r in range(4):
            rows = pl.ds(r * 256, 256)
            set_pair(rows, image_ref[rows, :] * root)

    def orthonormalise():
        pair = pair_ref[...]
        corr = dot_tn(pair, pair)
        corr = (corr[:RANK, :RANK] + corr[RANK:, RANK:]) + (corr[:RANK, RANK:] + corr[RANK:, :RANK])
        least = inverse_factor(corr, inv_ref)
        high, low = split_two(inv_ref[...])
        weights = jnp.concatenate(
            [jnp.concatenate([high, high], axis=1), jnp.concatenate([low, jnp.zeros_like(low)], axis=1)], axis=0
        )
        for r in range(4):
            rows = pl.ds(r * 256, 256)
            both = dot_nt(pair[r * 256 : (r + 1) * 256], weights)
            value = both[:, :RANK] + both[:, RANK:]
            image_ref[rows, :] = value
            set_pair(rows, value)
        return least

    def step(carry):
        i, stop = carry
        pl.when(jnp.logical_or(i == 0, i == ITERS))(start)
        multiply()
        least = lax.cond(i >= ITERS - 1, orthonormalise, lambda: jnp.float32(1.0))
        sound = least >= LEAST_PIVOT
        stop = jnp.where(jnp.logical_and(i == ITERS - 1, jnp.logical_not(sound)), 2 * ITERS, stop)
        return i + 1, stop

    lax.while_loop(lambda carry: carry[0] < carry[1], step, (jnp.int32(0), jnp.int32(ITERS)))

    own_rows = ROWS // SPLIT
    basis_ref[...] = image_ref[pl.ds(pl.multiple_of(lax.rem(mode * own_rows + core * 512, ROWS), own_rows), own_rows), :]
    total = jnp.zeros((RANK, cols), jnp.float32)
    for half in range(2):
        offset = pl.multiple_of(lax.rem(core * 512 + half * 512, ROWS), 512)
        total = total + dot_tn(pair_ref[pl.ds(half * 512, 512), :RANK], field_ref[pl.ds(offset, 512), :cols])
    core_ref[...] = total.reshape(core_ref.shape)


def on_device(unfolded, initial):
    held, cols = unfolded.shape[0], unfolded.shape[1] // SPLIT
    columns = unfolded.shape[1] * lax.axis_size("zh") * lax.axis_size("zl") * lax.axis_size("core")
    core, mode = lax.axis_index("core"), lax.axis_index(MODE)
    place = jnp.stack([core, mode]).astype(jnp.int32)
    vmem = pl.BlockSpec(memory_space=pltpu.VMEM)
    smem = pl.BlockSpec(memory_space=pltpu.SMEM)
    swap = [(0, 1), (1, 0)]

    high = lax.reduce_precision(initial, exponent_bits=8, mantissa_bits=7)
    half = jnp.where(core == 0, high, initial - high).astype(jnp.bfloat16)
    parts = jnp.concatenate(
        [
            unfolded.reshape(held, SPLIT, cols).transpose(1, 0, 2),
            jnp.broadcast_to(half[None], (SPLIT, held, RANK)),
        ],
        axis=2,
    )
    own = lax.all_to_all(parts, MODE, split_axis=0, concat_axis=0, tiled=True).reshape(ROWS, cols + RANK)
    twin = lax.ppermute(own, "core", swap)
    partial_gram = pl.pallas_call(
        gram_kernel,
        out_shape=jax.ShapeDtypeStruct((SPLIT, HALF_BLOCKS, SLIVER, BLOCK), jnp.float32),
        in_specs=[smem, vmem, vmem],
        out_specs=vmem,
        compiler_params=pltpu.CompilerParams(vmem_limit_bytes=16 * 1024 * 1024),
        name="gram",
    )(place, own, twin)

    got = lax.all_to_all(partial_gram, MODE, split_axis=0, concat_axis=0, tiled=True)
    sliver = jnp.sum(got, axis=0)
    got = jnp.broadcast_to(sliver[None], (lax.axis_size("zl"),) + sliver.shape)
    got = lax.all_to_all(got, "zl", split_axis=0, concat_axis=0, tiled=True)
    got = lax.all_gather(jnp.sum(got, axis=0), "zh", axis=0, tiled=False)
    sliver = jnp.sum(got, axis=0)
    got = jnp.broadcast_to(sliver[None], (SPLIT,) + sliver.shape)
    own_gram = lax.all_to_all(got, MODE, split_axis=0, concat_axis=0, tiled=True)
    twin_gram = lax.ppermute(own_gram, "core", swap)

    basis, core_rows = pl.pallas_call(
        lambda *refs: iterate_kernel(columns, cols, *refs),
        out_shape=(
            jax.ShapeDtypeStruct((held, RANK), jnp.float32),
            jax.ShapeDtypeStruct((SPLIT, RANK // SPLIT, cols), jnp.float32),
        ),
        in_specs=[smem, vmem, vmem, vmem, vmem],
        out_specs=(vmem, vmem),
        scratch_shapes=[
            pltpu.VMEM((ROWS, ROWS), jnp.bfloat16),
            pltpu.VMEM((ROWS, ROWS), jnp.bfloat16),
            pltpu.VMEM((ROWS, 2 * RANK), jnp.bfloat16),
            pltpu.VMEM((ROWS, RANK), jnp.float32),
            pltpu.VMEM((RANK, RANK), jnp.float32),
        ],
        compiler_params=pltpu.CompilerParams(vmem_limit_bytes=32 * 1024 * 1024),
        name="iterate",
    )(place, own_gram, twin_gram, own, twin)
    core_cols = lax.all_to_all(core_rows, MODE, split_axis=0, concat_axis=0, tiled=True)
    return basis, core_cols.transpose(1, 0, 2).reshape(RANK // SPLIT, SPLIT * cols)


def solution(mesh):
    chips = Mesh(mesh.devices.reshape(4, 4, 4, mesh.devices.shape[1] // 8, 2), ("y", "x", "zh", "zl", "core"))
    rest = ("zh", "zl", "core")
    in_specs = (P(MODE, rest), P(MODE, None))
    out_specs = (P(MODE, None), P(MODE, rest))
    return jax.shard_map(on_device, mesh=chips, in_specs=in_specs, out_specs=out_specs, check_vma=False)
```

```python
import jax
import jax.numpy as jnp
from jax import lax
from jax.experimental import pallas as pl
from jax.experimental.pallas import tpu as pltpu
from jax.sharding import Mesh, PartitionSpec as P

ITERS = 4
ROWS = 1024
RANK = 128
BLOCK = 128
HALF_BLOCKS = 18
SPLIT = 16
SLIVER = BLOCK // SPLIT
LEAST_PIVOT = 2e-3
CHUNK = 256
MODE = ("y", "x")

SLOTS = [(t, t + d) for t in range(4) for d in range(4)]


def split_two(value):
    high = value.astype(jnp.bfloat16)
    return high, (value - high.astype(jnp.float32)).astype(jnp.bfloat16)


def dot_nt(left, right):
    return lax.dot_general(left, right, (((1,), (1,)), ((), ())), preferred_element_type=jnp.float32)


def dot_tn(left, right):
    return lax.dot_general(left, right, (((0,), (0,)), ((), ())), preferred_element_type=jnp.float32)


def dot_nn(left, right):
    return jnp.dot(left, right, preferred_element_type=jnp.float32)


def gram_kernel(place_ref, own_ref, twin_ref, out_ref):
    core = place_ref[0]
    cols = own_ref.shape[1] - RANK

    def rows(ref, a):
        start = pl.multiple_of(lax.rem(core * 512 + a * 256, ROWS), 256)
        return ref[pl.ds(start, 256), :cols]

    own = [rows(own_ref, a) for a in range(4)]
    twin = [rows(twin_ref, a) for a in range(4)]
    tiles = {}
    for a, b in ((0, 0), (0, 1), (0, 2), (1, 1), (1, 2), (1, 3)):
        tiles[a, b] = dot_nt(own[a], own[b]) + dot_nt(twin[a], twin[b])

    def block(a, b):
        tile = tiles[a // 2, b // 2]
        return tile[(a % 2) * BLOCK : (a % 2 + 1) * BLOCK, (b % 2) * BLOCK : (b % 2 + 1) * BLOCK]

    for slot, (a, b) in enumerate(SLOTS):
        out_ref[:, slot] = block(a, b).reshape(SPLIT, SLIVER, BLOCK)
    for s in range(2):
        far = jnp.where(core == 0, block(s, s + 4), block(s + 2, s + 6))
        out_ref[:, 16 + s] = far.reshape(SPLIT, SLIVER, BLOCK)


def inverse_factor(corr, inv_ref):
    panels = RANK // 8
    row = lax.broadcasted_iota(jnp.int32, (8, RANK), 0)
    lane = lax.broadcasted_iota(jnp.int32, (8, RANK), 1)
    left = [corr[8 * p : 8 * p + 8, :] for p in range(panels)]
    right = [jnp.where(lane == row + 8 * p, 1.0, 0.0) for p in range(panels)]
    least = jnp.full((8, RANK), jnp.inf, jnp.float32)

    def columns_of(value, p):
        return [jnp.broadcast_to(value[:, 8 * p + k : 8 * p + k + 1], (8, RANK)) for k in range(8)]

    for p in range(panels):
        here, there = left[p], right[p]
        column = columns_of(here, p)
        pivots = jnp.zeros((8, RANK), jnp.float32)
        steps = []
        for k in range(0, 8, 2):
            first, second = column[k], column[k + 1]
            a, b, c = first[k : k + 1], first[k + 1 : k + 2], second[k + 1 : k + 2]
            det = a * c - b * b
            inv_a, inv_det = 1.0 / a, 1.0 / det
            ratio, inv_c = b * inv_a, a * inv_det
            pivots = jnp.where(row == k, a, jnp.where(row == k + 1, det * inv_a, pivots))
            lower = jnp.where(row > k, first, 0.0)
            lowest = jnp.where(row > k + 1, second - first * ratio, 0.0)

            def heads(value):
                one = value[k : k + 1]
                two = (value[k + 1 : k + 2] - ratio * one) * inv_c
                return one * inv_a, two

            tops = [heads(column[later]) for later in range(k + 2, 8)]
            for later, (one, two) in zip(range(k + 2, 8), tops):
                column[later] = column[later] - lower * one - lowest * two
            sides = heads(here), heads(there)
            here = here - lower * sides[0][0] - lowest * sides[0][1]
            there = there - lower * sides[1][0] - lowest * sides[1][1]
            steps.append((k, ratio, tops, sides))
        least = jnp.minimum(least, pivots)
        inv_ref[8 * p : 8 * p + 8, :] = there * lax.rsqrt(pivots)
        for q in range(p + 1, panels):
            column = columns_of(left[q], p)
            for k, ratio, tops, sides in steps:
                lower = column[k]
                lowest = column[k + 1] - lower * ratio
                for later, (one, two) in zip(range(k + 2, 8), tops):
                    column[later] = column[later] - lower * one - lowest * two
                left[q] = left[q] - lower * sides[0][0] - lowest * sides[0][1]
                right[q] = right[q] - lower * sides[1][0] - lowest * sides[1][1]
    return jnp.min(least)


def iterate_kernel(cols, place_ref, own_ref, twin_ref, field_ref, twin_field_ref, basis_ref, core_ref,
                   high_ref, low_ref, pair_ref, image_ref, inv_ref):
    core, mode = place_ref[0], place_ref[1]
    row = lax.broadcasted_iota(jnp.int32, (RANK, RANK), 0)
    diagonal = row == lax.broadcasted_iota(jnp.int32, (RANK, RANK), 1)
    largest = jnp.zeros((BLOCK, BLOCK), jnp.float32)

    def at(index):
        return pl.ds(index * BLOCK if isinstance(index, int) else pl.multiple_of(index * BLOCK, BLOCK), BLOCK)

    def put(a, b, value):
        high, low = split_two(value)
        high_ref[at(a), at(b)] = high
        low_ref[at(a), at(b)] = low
        if not (isinstance(a, int) and a == b):
            high, low = split_two(value.T)
            high_ref[at(b), at(a)] = high
            low_ref[at(b), at(a)] = low

    for slot, (a, b) in enumerate(SLOTS):
        for ref, shift in ((own_ref, 0), (twin_ref, 4)):
            value = ref[:, slot].reshape(BLOCK, BLOCK)
            if a == b:
                largest = jnp.maximum(largest, jnp.where(diagonal, value, 0.0))
            put((a + shift) % 8, (b + shift) % 8, value)
    for s in range(2):
        put(2 * core + s, 2 * core + s + 4, own_ref[:, 16 + s].reshape(BLOCK, BLOCK))
        put(6 - 2 * core + s, 2 - 2 * core + s, twin_ref[:, 16 + s].reshape(BLOCK, BLOCK))
    scale = 1.0 / jnp.max(largest)

    def set_pair(side, rows, value):
        high, low = split_two(value)
        pair_ref[side, rows, :RANK] = high
        pair_ref[side, rows, RANK:] = low

    def start():
        for half in range(2):
            offset = pl.multiple_of(lax.rem(core * 512 + half * 512, ROWS), 512)
            rows = pl.ds(half * 512, 512)
            first = field_ref[pl.ds(offset, 512), cols:]
            second = twin_field_ref[pl.ds(offset, 512), cols:]
            pair_ref[0, rows, :RANK] = jnp.where(core == 0, first, second)
            pair_ref[0, rows, RANK:] = jnp.where(core == 0, second, first)

    def multiply(side):
        for r in range(ROWS // CHUNK):
            rows = pl.ds(r * CHUNK, CHUNK)
            both = dot_nn(high_ref[rows, :], pair_ref[side])
            small = dot_nn(low_ref[rows, :], pair_ref[side, :, :RANK])
            set_pair(1 - side, rows, (both[:, :RANK] + (both[:, RANK:] + small)) * scale)

    def orthonormalise(side):
        corr = dot_tn(pair_ref[side], pair_ref[side])
        corr = (corr[:RANK, :RANK] + corr[RANK:, RANK:]) + (corr[:RANK, RANK:] + corr[RANK:, :RANK])
        squares = jnp.where(diagonal, corr, 0.0)
        across = lax.rsqrt(jnp.sum(squares, axis=0, keepdims=True))
        down = lax.rsqrt(jnp.sum(squares, axis=1, keepdims=True))
        least = inverse_factor(corr * across * down, inv_ref)
        high, low = split_two(inv_ref[...] * across)
        weights = jnp.concatenate(
            [jnp.concatenate([high, high], axis=1), jnp.concatenate([low, jnp.zeros_like(low)], axis=1)], axis=0
        )
        for r in range(4):
            rows = pl.ds(r * 256, 256)
            both = dot_nt(pair_ref[side, rows, :], weights)
            value = both[:, :RANK] + both[:, RANK:]
            image_ref[rows, :] = value
            set_pair(0, rows, value)
        return least

    def step(carry):
        i, stop = carry

        @pl.when(i == 0)
        def _():
            start()
            for n in range(ITERS):
                multiply(n % 2)

        @pl.when(i > 0)
        def _():
            pl.when(i == 1)(start)
            multiply(0)

        least = orthonormalise(jnp.where(i == 0, ITERS % 2, 1))
        sound = least >= LEAST_PIVOT
        return i + 1, jnp.where(jnp.logical_and(i == 0, jnp.logical_not(sound)), ITERS + 1, stop)

    lax.while_loop(lambda carry: carry[0] < carry[1], step, (jnp.int32(0), jnp.int32(1)))

    own_rows = ROWS // SPLIT
    basis_ref[...] = image_ref[pl.ds(pl.multiple_of(lax.rem(mode * own_rows + core * 512, ROWS), own_rows), own_rows), :]
    total = jnp.zeros((RANK, cols), jnp.float32)
    for half in range(2):
        offset = pl.multiple_of(lax.rem(core * 512 + half * 512, ROWS), 512)
        total = total + dot_tn(pair_ref[0, pl.ds(half * 512, 512), :RANK], field_ref[pl.ds(offset, 512), :cols])
    core_ref[...] = total.reshape(core_ref.shape)


def on_device(unfolded, initial):
    held, cols = unfolded.shape[0], unfolded.shape[1] // SPLIT
    core, mode = lax.axis_index("core"), lax.axis_index(MODE)
    place = jnp.stack([core, mode]).astype(jnp.int32)
    vmem = pl.BlockSpec(memory_space=pltpu.VMEM)
    smem = pl.BlockSpec(memory_space=pltpu.SMEM)
    swap = [(0, 1), (1, 0)]

    high = lax.reduce_precision(initial, exponent_bits=8, mantissa_bits=7)
    half = jnp.where(core == 0, high, initial - high).astype(jnp.bfloat16)
    parts = jnp.concatenate(
        [
            unfolded.reshape(held, SPLIT, cols).transpose(1, 0, 2),
            jnp.broadcast_to(half[None], (SPLIT, held, RANK)),
        ],
        axis=2,
    )
    own = lax.all_to_all(parts, MODE, split_axis=0, concat_axis=0, tiled=True).reshape(ROWS, cols + RANK)
    twin = lax.ppermute(own, "core", swap)
    partial_gram = pl.pallas_call(
        gram_kernel,
        out_shape=jax.ShapeDtypeStruct((SPLIT, HALF_BLOCKS, SLIVER, BLOCK), jnp.float32),
        in_specs=[smem, vmem, vmem],
        out_specs=vmem,
        compiler_params=pltpu.CompilerParams(vmem_limit_bytes=16 * 1024 * 1024),
        name="gram",
    )(place, own, twin)

    got = lax.all_to_all(partial_gram, MODE, split_axis=0, concat_axis=0, tiled=True)
    sliver = jnp.sum(got, axis=0)
    got = jnp.broadcast_to(sliver[None], (lax.axis_size("zl"),) + sliver.shape)
    got = lax.all_to_all(got, "zl", split_axis=0, concat_axis=0, tiled=True)
    got = lax.all_gather(jnp.sum(got, axis=0), "zh", axis=0, tiled=False)
    sliver = jnp.sum(got, axis=0)
    got = jnp.broadcast_to(sliver[None], (SPLIT,) + sliver.shape)
    own_gram = lax.all_to_all(got, MODE, split_axis=0, concat_axis=0, tiled=True)
    twin_gram = lax.ppermute(own_gram, "core", swap)

    basis, core_rows = pl.pallas_call(
        lambda *refs: iterate_kernel(cols, *refs),
        out_shape=(
            jax.ShapeDtypeStruct((held, RANK), jnp.float32),
            jax.ShapeDtypeStruct((SPLIT, RANK // SPLIT, cols), jnp.float32),
        ),
        in_specs=[smem, vmem, vmem, vmem, vmem],
        out_specs=(vmem, vmem),
        scratch_shapes=[
            pltpu.VMEM((ROWS, ROWS), jnp.bfloat16),
            pltpu.VMEM((ROWS, ROWS), jnp.bfloat16),
            pltpu.VMEM((2, ROWS, 2 * RANK), jnp.bfloat16),
            pltpu.VMEM((ROWS, RANK), jnp.float32),
            pltpu.VMEM((RANK, RANK), jnp.float32),
        ],
        compiler_params=pltpu.CompilerParams(vmem_limit_bytes=32 * 1024 * 1024),
        name="iterate",
    )(place, own_gram, twin_gram, own, twin)
    core_cols = lax.all_to_all(core_rows, MODE, split_axis=0, concat_axis=0, tiled=True)
    return basis, core_cols.transpose(1, 0, 2).reshape(RANK // SPLIT, SPLIT * cols)


def solution(mesh):
    chips = Mesh(mesh.devices.reshape(4, 4, 4, mesh.devices.shape[1] // 8, 2), ("y", "x", "zh", "zl", "core"))
    rest = ("zh", "zl", "core")
    in_specs = (P(MODE, rest), P(MODE, None))
    out_specs = (P(MODE, None), P(MODE, rest))
    return jax.shard_map(on_device, mesh=chips, in_specs=in_specs, out_specs=out_specs, check_vma=False)
```

```python
import jax
import jax.numpy as jnp
from jax import lax
from jax.experimental import pallas as pl
from jax.experimental.pallas import tpu as pltpu
from jax.sharding import Mesh, PartitionSpec as P

ITERS = 4
ROWS = 1024
RANK = 128
BLOCK = 128
HALF_BLOCKS = 18
SPLIT = 16
SLIVER = BLOCK // SPLIT
LEAST_PIVOT = 2e-3
CHUNK = 256
MODE = ("y", "x")
PLANES = ("y", "x", "z0")
PAIR = HALF_BLOCKS // 2

SLOTS = [(t, t + d) for t in range(4) for d in range(4)]


def split_two(value):
    high = value.astype(jnp.bfloat16)
    return high, (value - high.astype(jnp.float32)).astype(jnp.bfloat16)


def dot_nt(left, right):
    return lax.dot_general(left, right, (((1,), (1,)), ((), ())), preferred_element_type=jnp.float32)


def dot_tn(left, right):
    return lax.dot_general(left, right, (((0,), (0,)), ((), ())), preferred_element_type=jnp.float32)


def dot_nn(left, right):
    return jnp.dot(left, right, preferred_element_type=jnp.float32)


def gram_kernel(place_ref, own_ref, twin_ref, out_ref):
    core = place_ref[0]
    cols = own_ref.shape[1] - RANK

    def rows(ref, a):
        start = pl.multiple_of(lax.rem(core * 512 + a * 256, ROWS), 256)
        return ref[pl.ds(start, 256), :cols]

    own = [rows(own_ref, a) for a in range(4)]
    twin = [rows(twin_ref, a) for a in range(4)]
    tiles = {}
    for a, b in ((0, 0), (0, 1), (0, 2), (1, 1), (1, 2), (1, 3)):
        tiles[a, b] = dot_nt(own[a], own[b]) + dot_nt(twin[a], twin[b])

    def block(a, b):
        tile = tiles[a // 2, b // 2]
        return tile[(a % 2) * BLOCK : (a % 2 + 1) * BLOCK, (b % 2) * BLOCK : (b % 2 + 1) * BLOCK]

    for slot, (a, b) in enumerate(SLOTS):
        out_ref[:, slot // PAIR, slot % PAIR] = block(a, b).reshape(SPLIT, SLIVER, BLOCK)
    for s in range(2):
        far = jnp.where(core == 0, block(s, s + 4), block(s + 2, s + 6))
        out_ref[:, 1, PAIR - 2 + s] = far.reshape(SPLIT, SLIVER, BLOCK)


def inverse_factor(corr, inv_ref):
    panels = RANK // 8
    row = lax.broadcasted_iota(jnp.int32, (8, RANK), 0)
    lane = lax.broadcasted_iota(jnp.int32, (8, RANK), 1)
    left = [corr[8 * p : 8 * p + 8, :] for p in range(panels)]
    right = [jnp.where(lane == row + 8 * p, 1.0, 0.0) for p in range(panels)]
    least = jnp.full((8, RANK), jnp.inf, jnp.float32)

    def columns_of(value, p):
        return [jnp.broadcast_to(value[:, 8 * p + k : 8 * p + k + 1], (8, RANK)) for k in range(8)]

    for p in range(panels):
        here, there = left[p], right[p]
        column = columns_of(here, p)
        pivots = jnp.zeros((8, RANK), jnp.float32)
        steps = []
        for k in range(0, 8, 2):
            first, second = column[k], column[k + 1]
            a, b, c = first[k : k + 1], first[k + 1 : k + 2], second[k + 1 : k + 2]
            det = a * c - b * b
            inv_a, inv_det = 1.0 / a, 1.0 / det
            ratio, inv_c = b * inv_a, a * inv_det
            pivots = jnp.where(row == k, a, jnp.where(row == k + 1, det * inv_a, pivots))
            lower = jnp.where(row > k, first, 0.0)
            lowest = jnp.where(row > k + 1, second - first * ratio, 0.0)

            def heads(value):
                one = value[k : k + 1]
                two = (value[k + 1 : k + 2] - ratio * one) * inv_c
                return one * inv_a, two

            tops = [heads(column[later]) for later in range(k + 2, 8)]
            for later, (one, two) in zip(range(k + 2, 8), tops):
                column[later] = column[later] - lower * one - lowest * two
            sides = heads(here), heads(there)
            here = here - lower * sides[0][0] - lowest * sides[0][1]
            there = there - lower * sides[1][0] - lowest * sides[1][1]
            steps.append((k, ratio, tops, sides))
        least = jnp.minimum(least, pivots)
        inv_ref[8 * p : 8 * p + 8, :] = there * lax.rsqrt(pivots)
        for q in range(p + 1, panels):
            column = columns_of(left[q], p)
            for k, ratio, tops, sides in steps:
                lower = column[k]
                lowest = column[k + 1] - lower * ratio
                for later, (one, two) in zip(range(k + 2, 8), tops):
                    column[later] = column[later] - lower * one - lowest * two
                left[q] = left[q] - lower * sides[0][0] - lowest * sides[0][1]
                right[q] = right[q] - lower * sides[1][0] - lowest * sides[1][1]
    return jnp.min(least)


def iterate_kernel(cols, place_ref, own_ref, twin_ref, field_ref, twin_field_ref, basis_ref, core_ref,
                   high_ref, low_ref, pair_ref, image_ref, inv_ref):
    core, mode = place_ref[0], place_ref[1]
    row = lax.broadcasted_iota(jnp.int32, (RANK, RANK), 0)
    diagonal = row == lax.broadcasted_iota(jnp.int32, (RANK, RANK), 1)
    largest = jnp.zeros((BLOCK, BLOCK), jnp.float32)

    def at(index):
        return pl.ds(index * BLOCK if isinstance(index, int) else pl.multiple_of(index * BLOCK, BLOCK), BLOCK)

    def put(a, b, value):
        high, low = split_two(value)
        high_ref[at(a), at(b)] = high
        low_ref[at(a), at(b)] = low
        if not (isinstance(a, int) and a == b):
            high, low = split_two(value.T)
            high_ref[at(b), at(a)] = high
            low_ref[at(b), at(a)] = low

    for slot, (a, b) in enumerate(SLOTS):
        for ref, shift in ((own_ref, 0), (twin_ref, 4)):
            value = ref[:, slot // PAIR, slot % PAIR].reshape(BLOCK, BLOCK)
            if a == b:
                largest = jnp.maximum(largest, jnp.where(diagonal, value, 0.0))
            put((a + shift) % 8, (b + shift) % 8, value)
    for s in range(2):
        put(2 * core + s, 2 * core + s + 4, own_ref[:, 1, PAIR - 2 + s].reshape(BLOCK, BLOCK))
        put(6 - 2 * core + s, 2 - 2 * core + s, twin_ref[:, 1, PAIR - 2 + s].reshape(BLOCK, BLOCK))
    scale = 1.0 / jnp.max(largest)

    def set_pair(side, rows, value):
        high, low = split_two(value)
        pair_ref[side, rows, :RANK] = high
        pair_ref[side, rows, RANK:] = low

    def start():
        for half in range(2):
            offset = pl.multiple_of(lax.rem(core * 512 + half * 512, ROWS), 512)
            rows = pl.ds(half * 512, 512)
            first = field_ref[pl.ds(offset, 512), cols:]
            second = twin_field_ref[pl.ds(offset, 512), cols:]
            pair_ref[0, rows, :RANK] = jnp.where(core == 0, first, second)
            pair_ref[0, rows, RANK:] = jnp.where(core == 0, second, first)

    def multiply(side):
        for r in range(ROWS // CHUNK):
            rows = pl.ds(r * CHUNK, CHUNK)
            both = dot_nn(high_ref[rows, :], pair_ref[side])
            small = dot_nn(low_ref[rows, :], pair_ref[side, :, :RANK])
            set_pair(1 - side, rows, (both[:, :RANK] + (both[:, RANK:] + small)) * scale)

    def orthonormalise(side):
        corr = dot_tn(pair_ref[side], pair_ref[side])
        corr = (corr[:RANK, :RANK] + corr[RANK:, RANK:]) + (corr[:RANK, RANK:] + corr[RANK:, :RANK])
        squares = jnp.where(diagonal, corr, 0.0)
        across = lax.rsqrt(jnp.sum(squares, axis=0, keepdims=True))
        down = lax.rsqrt(jnp.sum(squares, axis=1, keepdims=True))
        least = inverse_factor(corr * across * down, inv_ref)
        high, low = split_two(inv_ref[...] * across)
        weights = jnp.concatenate(
            [jnp.concatenate([high, high], axis=1), jnp.concatenate([low, jnp.zeros_like(low)], axis=1)], axis=0
        )
        for r in range(4):
            rows = pl.ds(r * 256, 256)
            both = dot_nt(pair_ref[side, rows, :], weights)
            value = both[:, :RANK] + both[:, RANK:]
            image_ref[rows, :] = value
            set_pair(0, rows, value)
        return least

    def step(carry):
        i, stop = carry

        @pl.when(i == 0)
        def _():
            start()
            for n in range(ITERS):
                multiply(n % 2)

        @pl.when(i > 0)
        def _():
            pl.when(i == 1)(start)
            multiply(0)

        least = orthonormalise(jnp.where(i == 0, ITERS % 2, 1))
        sound = least >= LEAST_PIVOT
        return i + 1, jnp.where(jnp.logical_and(i == 0, jnp.logical_not(sound)), ITERS + 1, stop)

    lax.while_loop(lambda carry: carry[0] < carry[1], step, (jnp.int32(0), jnp.int32(1)))

    own_rows = ROWS // SPLIT
    basis_ref[...] = image_ref[pl.ds(pl.multiple_of(lax.rem(mode * own_rows + core * 512, ROWS), own_rows), own_rows), :]
    total = jnp.zeros((RANK, cols), jnp.float32)
    for half in range(2):
        offset = pl.multiple_of(lax.rem(core * 512 + half * 512, ROWS), 512)
        total = total + dot_tn(pair_ref[0, pl.ds(half * 512, 512), :RANK], field_ref[pl.ds(offset, 512), :cols])
    core_ref[...] = total.reshape(core_ref.shape)


def on_device(unfolded, initial):
    held, cols = unfolded.shape[0], unfolded.shape[1] // SPLIT
    core, mode = lax.axis_index("core"), lax.axis_index(MODE)
    place = jnp.stack([core, mode]).astype(jnp.int32)
    vmem = pl.BlockSpec(memory_space=pltpu.VMEM)
    smem = pl.BlockSpec(memory_space=pltpu.SMEM)
    swap = [(0, 1), (1, 0)]

    high = lax.reduce_precision(initial, exponent_bits=8, mantissa_bits=7)
    half = jnp.where(core == 0, high, initial - high).astype(jnp.bfloat16)
    parts = jnp.concatenate(
        [
            unfolded.reshape(held, SPLIT, cols).transpose(1, 0, 2),
            jnp.broadcast_to(half[None], (SPLIT, held, RANK)),
        ],
        axis=2,
    )
    own = lax.all_to_all(parts, MODE, split_axis=0, concat_axis=0, tiled=True).reshape(ROWS, cols + RANK)
    twin = lax.ppermute(own, "core", swap)
    partial_gram = pl.pallas_call(
        gram_kernel,
        out_shape=jax.ShapeDtypeStruct((SPLIT, 2, PAIR, SLIVER, BLOCK), jnp.float32),
        in_specs=[smem, vmem, vmem],
        out_specs=vmem,
        compiler_params=pltpu.CompilerParams(vmem_limit_bytes=16 * 1024 * 1024),
        name="gram",
    )(place, own, twin)

    partial_gram = partial_gram.reshape(2 * SPLIT, PAIR, SLIVER, BLOCK)
    got = lax.all_to_all(partial_gram, PLANES, split_axis=0, concat_axis=0, tiled=True)
    sliver = jnp.sum(got, axis=0)
    for axis in ("z1", "zh"):
        sliver = jnp.sum(lax.all_gather(sliver, axis, axis=0, tiled=False), axis=0)
    got = jnp.broadcast_to(sliver[None], got.shape)
    own_gram = lax.all_to_all(got, PLANES, split_axis=0, concat_axis=0, tiled=True)
    own_gram = own_gram.reshape(SPLIT, 2, PAIR, SLIVER, BLOCK)
    twin_gram = lax.ppermute(own_gram, "core", swap)

    basis, core_rows = pl.pallas_call(
        lambda *refs: iterate_kernel(cols, *refs),
        out_shape=(
            jax.ShapeDtypeStruct((held, RANK), jnp.float32),
            jax.ShapeDtypeStruct((SPLIT, RANK // SPLIT, cols), jnp.float32),
        ),
        in_specs=[smem, vmem, vmem, vmem, vmem],
        out_specs=(vmem, vmem),
        scratch_shapes=[
            pltpu.VMEM((ROWS, ROWS), jnp.bfloat16),
            pltpu.VMEM((ROWS, ROWS), jnp.bfloat16),
            pltpu.VMEM((2, ROWS, 2 * RANK), jnp.bfloat16),
            pltpu.VMEM((ROWS, RANK), jnp.float32),
            pltpu.VMEM((RANK, RANK), jnp.float32),
        ],
        compiler_params=pltpu.CompilerParams(vmem_limit_bytes=32 * 1024 * 1024),
        name="iterate",
    )(place, own_gram, twin_gram, own, twin)
    core_cols = lax.all_to_all(core_rows, MODE, split_axis=0, concat_axis=0, tiled=True)
    return basis, core_cols.transpose(1, 0, 2).reshape(RANK // SPLIT, SPLIT * cols)


def solution(mesh):
    chips = Mesh(mesh.devices.reshape(4, 4, mesh.devices.shape[1] // 8, 2, 2, 2), ("y", "x", "zh", "z1", "z0", "core"))
    rest = ("zh", "z1", "z0", "core")
    in_specs = (P(MODE, rest), P(MODE, None))
    out_specs = (P(MODE, None), P(MODE, rest))
    return jax.shard_map(on_device, mesh=chips, in_specs=in_specs, out_specs=out_specs, check_vma=False)
```

```python
import jax
import jax.numpy as jnp
from jax import lax
from jax.experimental import pallas as pl
from jax.experimental.pallas import tpu as pltpu
from jax.sharding import Mesh, PartitionSpec as P

ITERS = 4
ROWS = 1024
RANK = 128
BLOCK = 128
HALF_BLOCKS = 18
SPLIT = 16
SLIVER = BLOCK // SPLIT
LEAST_PIVOT = 2e-3
CHUNK = 256
MODE = ("y", "x")
PLANES = ("y", "x", "z0")
PAIR = HALF_BLOCKS // 2
HALF_TOP = 14.0

SLOTS = [(t, t + d) for t in range(4) for d in range(4)]


def split_two(value):
    high = value.astype(jnp.bfloat16)
    return high, (value - high.astype(jnp.float32)).astype(jnp.bfloat16)


def dot_nt(left, right):
    return lax.dot_general(left, right, (((1,), (1,)), ((), ())), preferred_element_type=jnp.float32)


def dot_tn(left, right):
    return lax.dot_general(left, right, (((0,), (0,)), ((), ())), preferred_element_type=jnp.float32)


def dot_nn(left, right):
    return jnp.dot(left, right, preferred_element_type=jnp.float32)


def gram_kernel(place_ref, own_ref, twin_ref, out_ref):
    core = place_ref[0]
    cols = own_ref.shape[1] - RANK

    def rows(ref, a):
        start = pl.multiple_of(lax.rem(core * 512 + a * 256, ROWS), 256)
        return ref[pl.ds(start, 256), :cols]

    own = [rows(own_ref, a) for a in range(4)]
    twin = [rows(twin_ref, a) for a in range(4)]
    tiles = {}
    for a, b in ((0, 0), (0, 1), (0, 2), (1, 1), (1, 2), (1, 3)):
        tiles[a, b] = dot_nt(own[a], own[b]) + dot_nt(twin[a], twin[b])

    def block(a, b):
        tile = tiles[a // 2, b // 2]
        return tile[(a % 2) * BLOCK : (a % 2 + 1) * BLOCK, (b % 2) * BLOCK : (b % 2 + 1) * BLOCK]

    blocks = [block(a, b) for a, b in SLOTS]
    blocks += [jnp.where(core == 0, block(s, s + 4), block(s + 2, s + 6)) for s in range(2)]
    largest = jnp.abs(blocks[0])
    for value in blocks[1:]:
        largest = jnp.maximum(largest, jnp.abs(value))
    largest = jnp.maximum(jnp.max(largest, axis=(0, 1), keepdims=True), 1e-30)
    power = jnp.round(jnp.log2(largest))
    scale = jnp.exp2(HALF_TOP - power)
    for slot, value in enumerate(blocks):
        value = (value * scale).reshape(SPLIT, SLIVER, BLOCK)
        out_ref[:, slot // PAIR, slot % PAIR] = value.astype(out_ref.dtype)
    power = jnp.broadcast_to(power, (SPLIT, SLIVER, BLOCK))
    for plane in range(2):
        out_ref[:, plane, PAIR] = power.astype(out_ref.dtype)


def inverse_factor(corr, inv_ref):
    panels = RANK // 8
    row = lax.broadcasted_iota(jnp.int32, (8, RANK), 0)
    lane = lax.broadcasted_iota(jnp.int32, (8, RANK), 1)
    left = [corr[8 * p : 8 * p + 8, :] for p in range(panels)]
    right = [jnp.where(lane == row + 8 * p, 1.0, 0.0) for p in range(panels)]
    least = jnp.full((8, RANK), jnp.inf, jnp.float32)

    def columns_of(value, p):
        return [jnp.broadcast_to(value[:, 8 * p + k : 8 * p + k + 1], (8, RANK)) for k in range(8)]

    for p in range(panels):
        here, there = left[p], right[p]
        column = columns_of(here, p)
        pivots = jnp.zeros((8, RANK), jnp.float32)
        steps = []
        for k in range(0, 8, 2):
            first, second = column[k], column[k + 1]
            a, b, c = first[k : k + 1], first[k + 1 : k + 2], second[k + 1 : k + 2]
            det = a * c - b * b
            inv_a, inv_det = 1.0 / a, 1.0 / det
            ratio, inv_c = b * inv_a, a * inv_det
            pivots = jnp.where(row == k, a, jnp.where(row == k + 1, det * inv_a, pivots))
            lower = jnp.where(row > k, first, 0.0)
            lowest = jnp.where(row > k + 1, second - first * ratio, 0.0)

            def heads(value):
                one = value[k : k + 1]
                two = (value[k + 1 : k + 2] - ratio * one) * inv_c
                return one * inv_a, two

            tops = [heads(column[later]) for later in range(k + 2, 8)]
            for later, (one, two) in zip(range(k + 2, 8), tops):
                column[later] = column[later] - lower * one - lowest * two
            sides = heads(here), heads(there)
            here = here - lower * sides[0][0] - lowest * sides[0][1]
            there = there - lower * sides[1][0] - lowest * sides[1][1]
            steps.append((k, ratio, tops, sides))
        least = jnp.minimum(least, pivots)
        inv_ref[8 * p : 8 * p + 8, :] = there * lax.rsqrt(pivots)
        for q in range(p + 1, panels):
            column = columns_of(left[q], p)
            for k, ratio, tops, sides in steps:
                lower = column[k]
                lowest = column[k + 1] - lower * ratio
                for later, (one, two) in zip(range(k + 2, 8), tops):
                    column[later] = column[later] - lower * one - lowest * two
                left[q] = left[q] - lower * sides[0][0] - lowest * sides[0][1]
                right[q] = right[q] - lower * sides[1][0] - lowest * sides[1][1]
    return jnp.min(least)


def iterate_kernel(cols, place_ref, own_ref, twin_ref, field_ref, twin_field_ref, basis_ref, core_ref,
                   high_ref, low_ref, pair_ref, image_ref, inv_ref):
    core, mode = place_ref[0], place_ref[1]
    row = lax.broadcasted_iota(jnp.int32, (RANK, RANK), 0)
    diagonal = row == lax.broadcasted_iota(jnp.int32, (RANK, RANK), 1)
    largest = jnp.zeros((BLOCK, BLOCK), jnp.float32)

    def at(index):
        return pl.ds(index * BLOCK if isinstance(index, int) else pl.multiple_of(index * BLOCK, BLOCK), BLOCK)

    def put(a, b, value):
        high, low = split_two(value)
        high_ref[at(a), at(b)] = high
        low_ref[at(a), at(b)] = low
        if not (isinstance(a, int) and a == b):
            high, low = split_two(value.T)
            high_ref[at(b), at(a)] = high
            low_ref[at(b), at(a)] = low

    for slot, (a, b) in enumerate(SLOTS):
        for ref, shift in ((own_ref, 0), (twin_ref, 4)):
            value = ref[:, slot // PAIR, slot % PAIR].reshape(BLOCK, BLOCK)
            if a == b:
                largest = jnp.maximum(largest, jnp.where(diagonal, value, 0.0))
            put((a + shift) % 8, (b + shift) % 8, value)
    for s in range(2):
        put(2 * core + s, 2 * core + s + 4, own_ref[:, 1, PAIR - 2 + s].reshape(BLOCK, BLOCK))
        put(6 - 2 * core + s, 2 - 2 * core + s, twin_ref[:, 1, PAIR - 2 + s].reshape(BLOCK, BLOCK))
    scale = 1.0 / jnp.max(largest)

    def set_pair(side, rows, value):
        high, low = split_two(value)
        pair_ref[side, rows, :RANK] = high
        pair_ref[side, rows, RANK:] = low

    def start():
        for half in range(2):
            offset = pl.multiple_of(lax.rem(core * 512 + half * 512, ROWS), 512)
            rows = pl.ds(half * 512, 512)
            first = field_ref[pl.ds(offset, 512), cols:]
            second = twin_field_ref[pl.ds(offset, 512), cols:]
            pair_ref[0, rows, :RANK] = jnp.where(core == 0, first, second)
            pair_ref[0, rows, RANK:] = jnp.where(core == 0, second, first)

    def multiply(side):
        for r in range(ROWS // CHUNK):
            rows = pl.ds(r * CHUNK, CHUNK)
            both = dot_nn(high_ref[rows, :], pair_ref[side])
            small = dot_nn(low_ref[rows, :], pair_ref[side, :, :RANK])
            set_pair(1 - side, rows, (both[:, :RANK] + (both[:, RANK:] + small)) * scale)

    def orthonormalise(side):
        corr = dot_tn(pair_ref[side], pair_ref[side])
        corr = (corr[:RANK, :RANK] + corr[RANK:, RANK:]) + (corr[:RANK, RANK:] + corr[RANK:, :RANK])
        squares = jnp.where(diagonal, corr, 0.0)
        across = lax.rsqrt(jnp.sum(squares, axis=0, keepdims=True))
        down = lax.rsqrt(jnp.sum(squares, axis=1, keepdims=True))
        least = inverse_factor(corr * across * down, inv_ref)
        high, low = split_two(inv_ref[...] * across)
        weights = jnp.concatenate(
            [jnp.concatenate([high, high], axis=1), jnp.concatenate([low, jnp.zeros_like(low)], axis=1)], axis=0
        )
        for r in range(4):
            rows = pl.ds(r * 256, 256)
            both = dot_nt(pair_ref[side, rows, :], weights)
            value = both[:, :RANK] + both[:, RANK:]
            image_ref[rows, :] = value
            set_pair(0, rows, value)
        return least

    def step(carry):
        i, stop = carry

        @pl.when(i == 0)
        def _():
            start()
            for n in range(ITERS):
                multiply(n % 2)

        @pl.when(i > 0)
        def _():
            pl.when(i == 1)(start)
            multiply(0)

        least = orthonormalise(jnp.where(i == 0, ITERS % 2, 1))
        sound = least >= LEAST_PIVOT
        return i + 1, jnp.where(jnp.logical_and(i == 0, jnp.logical_not(sound)), ITERS + 1, stop)

    lax.while_loop(lambda carry: carry[0] < carry[1], step, (jnp.int32(0), jnp.int32(1)))

    own_rows = ROWS // SPLIT
    basis_ref[...] = image_ref[pl.ds(pl.multiple_of(lax.rem(mode * own_rows + core * 512, ROWS), own_rows), own_rows), :]
    total = jnp.zeros((RANK, cols), jnp.float32)
    for half in range(2):
        offset = pl.multiple_of(lax.rem(core * 512 + half * 512, ROWS), 512)
        total = total + dot_tn(pair_ref[0, pl.ds(half * 512, 512), :RANK], field_ref[pl.ds(offset, 512), :cols])
    core_ref[...] = total.reshape(core_ref.shape)


def on_device(unfolded, initial):
    held, cols = unfolded.shape[0], unfolded.shape[1] // SPLIT
    core, mode = lax.axis_index("core"), lax.axis_index(MODE)
    place = jnp.stack([core, mode]).astype(jnp.int32)
    vmem = pl.BlockSpec(memory_space=pltpu.VMEM)
    smem = pl.BlockSpec(memory_space=pltpu.SMEM)
    swap = [(0, 1), (1, 0)]

    high = lax.reduce_precision(initial, exponent_bits=8, mantissa_bits=7)
    half = jnp.where(core == 0, high, initial - high).astype(jnp.bfloat16)
    parts = jnp.concatenate(
        [
            unfolded.reshape(held, SPLIT, cols).transpose(1, 0, 2),
            jnp.broadcast_to(half[None], (SPLIT, held, RANK)),
        ],
        axis=2,
    )
    own = lax.all_to_all(parts, MODE, split_axis=0, concat_axis=0, tiled=True).reshape(ROWS, cols + RANK)
    twin = lax.ppermute(own, "core", swap)
    partial_gram = pl.pallas_call(
        gram_kernel,
        out_shape=jax.ShapeDtypeStruct((SPLIT, 2, PAIR + 1, SLIVER, BLOCK), jnp.float32),
        in_specs=[smem, vmem, vmem],
        out_specs=vmem,
        compiler_params=pltpu.CompilerParams(vmem_limit_bytes=16 * 1024 * 1024),
        name="gram",
    )(place, own, twin)

    partial_gram = partial_gram.astype(jnp.float16).reshape(2 * SPLIT, (PAIR + 1) * SLIVER, BLOCK)
    got = lax.all_to_all(partial_gram, PLANES, split_axis=0, concat_axis=0, tiled=True)
    got = got.astype(jnp.float32).reshape(2 * SPLIT, PAIR + 1, SLIVER, BLOCK)
    sliver = jnp.sum(got[:, :PAIR] * jnp.exp2(got[:, PAIR:] - HALF_TOP), axis=0)
    for axis in ("z1", "zh"):
        sliver = jnp.sum(lax.all_gather(sliver, axis, axis=0, tiled=False), axis=0)
    got = jnp.broadcast_to(sliver[None], (2 * SPLIT,) + sliver.shape)
    own_gram = lax.all_to_all(got, PLANES, split_axis=0, concat_axis=0, tiled=True)
    own_gram = own_gram.reshape(SPLIT, 2, PAIR, SLIVER, BLOCK)
    twin_gram = lax.ppermute(own_gram, "core", swap)

    basis, core_rows = pl.pallas_call(
        lambda *refs: iterate_kernel(cols, *refs),
        out_shape=(
            jax.ShapeDtypeStruct((held, RANK), jnp.float32),
            jax.ShapeDtypeStruct((SPLIT, RANK // SPLIT, cols), jnp.float32),
        ),
        in_specs=[smem, vmem, vmem, vmem, vmem],
        out_specs=(vmem, vmem),
        scratch_shapes=[
            pltpu.VMEM((ROWS, ROWS), jnp.bfloat16),
            pltpu.VMEM((ROWS, ROWS), jnp.bfloat16),
            pltpu.VMEM((2, ROWS, 2 * RANK), jnp.bfloat16),
            pltpu.VMEM((ROWS, RANK), jnp.float32),
            pltpu.VMEM((RANK, RANK), jnp.float32),
        ],
        compiler_params=pltpu.CompilerParams(vmem_limit_bytes=32 * 1024 * 1024),
        name="iterate",
    )(place, own_gram, twin_gram, own, twin)
    core_cols = lax.all_to_all(core_rows, MODE, split_axis=0, concat_axis=0, tiled=True)
    return basis, core_cols.transpose(1, 0, 2).reshape(RANK // SPLIT, SPLIT * cols)


def solution(mesh):
    chips = Mesh(mesh.devices.reshape(4, 4, mesh.devices.shape[1] // 8, 2, 2, 2), ("y", "x", "zh", "z1", "z0", "core"))
    rest = ("zh", "z1", "z0", "core")
    in_specs = (P(MODE, rest), P(MODE, None))
    out_specs = (P(MODE, None), P(MODE, rest))
    return jax.shard_map(on_device, mesh=chips, in_specs=in_specs, out_specs=out_specs, check_vma=False)
```

```python
import jax
import jax.numpy as jnp
from jax import lax
from jax.experimental import pallas as pl
from jax.experimental.pallas import tpu as pltpu
from jax.sharding import Mesh, PartitionSpec as P

ITERS = 4
ROWS = 1024
RANK = 128
BLOCK = 128
HALF_BLOCKS = 18
SPLIT = 16
SLIVER = BLOCK // SPLIT
LEAST_PIVOT = 2e-3
CHUNK = 256
MODE = ("y", "x")
PLANES = ("y", "x", "z0")
PAIR = HALF_BLOCKS // 2
SHARE = ROWS // SPLIT // 4
HALF_TOP = 14.0

SLOTS = [(t, t + d) for t in range(4) for d in range(4)]


def split_two(value):
    high = value.astype(jnp.bfloat16)
    return high, (value - high.astype(jnp.float32)).astype(jnp.bfloat16)


def dot_nt(left, right):
    return lax.dot_general(left, right, (((1,), (1,)), ((), ())), preferred_element_type=jnp.float32)


def dot_tn(left, right):
    return lax.dot_general(left, right, (((0,), (0,)), ((), ())), preferred_element_type=jnp.float32)


def dot_nn(left, right):
    return jnp.dot(left, right, preferred_element_type=jnp.float32)


def gram_kernel(place_ref, own_ref, twin_ref, initial_ref, out_ref, share_ref):
    core, quarter = place_ref[0], place_ref[2]
    rows_sent = pl.ds(pl.multiple_of(quarter * SHARE, SHARE), SHARE)
    share_ref[...] = initial_ref[rows_sent, :].reshape(share_ref.shape)

    def rows(ref, a):
        start = pl.multiple_of(lax.rem(core * 512 + a * 256, ROWS), 256)
        return ref[pl.ds(start, 256), :]

    own = [rows(own_ref, a) for a in range(4)]
    twin = [rows(twin_ref, a) for a in range(4)]
    tiles = {}
    for a, b in ((0, 0), (0, 1), (0, 2), (1, 1), (1, 2), (1, 3)):
        tiles[a, b] = dot_nt(own[a], own[b]) + dot_nt(twin[a], twin[b])

    def block(a, b):
        tile = tiles[a // 2, b // 2]
        return tile[(a % 2) * BLOCK : (a % 2 + 1) * BLOCK, (b % 2) * BLOCK : (b % 2 + 1) * BLOCK]

    blocks = [block(a, b) for a, b in SLOTS]
    blocks += [jnp.where(core == 0, block(s, s + 4), block(s + 2, s + 6)) for s in range(2)]
    largest = jnp.abs(blocks[0])
    for value in blocks[1:]:
        largest = jnp.maximum(largest, jnp.abs(value))
    largest = jnp.maximum(jnp.max(largest, axis=(0, 1), keepdims=True), 1e-30)
    power = jnp.round(jnp.log2(largest))
    scale = jnp.exp2(HALF_TOP - power)
    for slot, value in enumerate(blocks):
        value = (value * scale).reshape(SPLIT, SLIVER, BLOCK)
        out_ref[:, slot // PAIR, slot % PAIR] = value.astype(out_ref.dtype)
    power = jnp.broadcast_to(power, (SPLIT, SLIVER, BLOCK))
    for plane in range(2):
        out_ref[:, plane, PAIR] = power.astype(out_ref.dtype)


def inverse_factor(corr, inv_ref):
    panels = RANK // 8
    row = lax.broadcasted_iota(jnp.int32, (8, RANK), 0)
    lane = lax.broadcasted_iota(jnp.int32, (8, RANK), 1)
    rows = [corr[8 * p : 8 * p + 8, :] for p in range(panels)]
    least = jnp.full((8, RANK), jnp.inf, jnp.float32)

    def columns_of(value, p):
        return [jnp.broadcast_to(value[:, 8 * p + k : 8 * p + k + 1], (8, RANK)) for k in range(8)]

    for p in range(panels):
        inside = jnp.logical_and(lane >= 8 * p, lane < 8 * p + 8)
        column = columns_of(rows[p], p)
        here = jnp.where(inside, jnp.where(lane == row + 8 * p, 1.0, 0.0), rows[p])
        pivots = jnp.zeros((8, RANK), jnp.float32)
        steps = []
        for k in range(0, 8, 2):
            first, second = column[k], column[k + 1]
            a, b, c = first[k : k + 1], first[k + 1 : k + 2], second[k + 1 : k + 2]
            det = a * c - b * b
            inv_a, inv_det = 1.0 / a, 1.0 / det
            ratio, inv_c = b * inv_a, a * inv_det
            pivots = jnp.where(row == k, a, jnp.where(row == k + 1, det * inv_a, pivots))
            lower = jnp.where(row > k, first, 0.0)
            lowest = jnp.where(row > k + 1, second - first * ratio, 0.0)

            def heads(value):
                one = value[k : k + 1]
                two = (value[k + 1 : k + 2] - ratio * one) * inv_c
                return one * inv_a, two

            tops = [heads(column[later]) for later in range(k + 2, 8)]
            for later, (one, two) in zip(range(k + 2, 8), tops):
                column[later] = column[later] - lower * one - lowest * two
            side = heads(here)
            here = here - lower * side[0] - lowest * side[1]
            steps.append((k, ratio, tops, side))
        least = jnp.minimum(least, pivots)
        inv_ref[8 * p : 8 * p + 8, :] = jnp.where(lane < 8 * p + 8, here * lax.rsqrt(pivots), 0.0)
        for q in range(p + 1, panels):
            column = columns_of(rows[q], p)
            value = jnp.where(inside, 0.0, rows[q])
            for k, ratio, tops, side in steps:
                lower = column[k]
                lowest = column[k + 1] - lower * ratio
                for later, (one, two) in zip(range(k + 2, 8), tops):
                    column[later] = column[later] - lower * one - lowest * two
                value = value - lower * side[0] - lowest * side[1]
            rows[q] = value
    return jnp.min(least)


def iterate_kernel(place_ref, own_ref, twin_ref, field_ref, basis_ref, core_ref,
                   high_ref, low_ref, pair_ref, image_ref, inv_ref):
    core, mode = place_ref[0], place_ref[1]
    row = lax.broadcasted_iota(jnp.int32, (RANK, RANK), 0)
    diagonal = row == lax.broadcasted_iota(jnp.int32, (RANK, RANK), 1)
    largest = jnp.zeros((BLOCK, BLOCK), jnp.float32)

    def at(index):
        return pl.ds(index * BLOCK if isinstance(index, int) else pl.multiple_of(index * BLOCK, BLOCK), BLOCK)

    def put(a, b, value):
        high, low = split_two(value)
        high_ref[at(a), at(b)] = high
        low_ref[at(a), at(b)] = low
        if not (isinstance(a, int) and a == b):
            high, low = split_two(value.T)
            high_ref[at(b), at(a)] = high
            low_ref[at(b), at(a)] = low

    for slot, (a, b) in enumerate(SLOTS):
        for ref, shift in ((own_ref, 0), (twin_ref, 4)):
            value = ref[:, slot // PAIR, slot % PAIR].reshape(BLOCK, BLOCK)
            if a == b:
                largest = jnp.maximum(largest, jnp.where(diagonal, value, 0.0))
            put((a + shift) % 8, (b + shift) % 8, value)
    for s in range(2):
        put(2 * core + s, 2 * core + s + 4, own_ref[:, 1, PAIR - 2 + s].reshape(BLOCK, BLOCK))
        put(6 - 2 * core + s, 2 - 2 * core + s, twin_ref[:, 1, PAIR - 2 + s].reshape(BLOCK, BLOCK))
    scale = 1.0 / jnp.max(largest)

    def set_pair(side, rows, value):
        high, low = split_two(value)
        pair_ref[side, rows, :RANK] = high
        pair_ref[side, rows, RANK:] = low

    def start():
        for m in range(SPLIT):
            for plane in range(2):
                for ref, part in ((own_ref, core), (twin_ref, 1 - core)):
                    begin = m * (ROWS // SPLIT) + plane * 2 * SHARE + part * SHARE - core * 512 + ROWS
                    rows = pl.ds(pl.multiple_of(lax.rem(begin, ROWS), SHARE), SHARE)
                    set_pair(0, rows, ref[m, plane, PAIR:].reshape(SHARE, RANK))

    def multiply(side):
        for r in range(ROWS // CHUNK):
            rows = pl.ds(r * CHUNK, CHUNK)
            both = dot_nn(high_ref[rows, :], pair_ref[side])
            small = dot_nn(low_ref[rows, :], pair_ref[side, :, :RANK])
            set_pair(1 - side, rows, (both[:, :RANK] + (both[:, RANK:] + small)) * scale)

    def orthonormalise(side):
        corr = dot_tn(pair_ref[side], pair_ref[side])
        corr = (corr[:RANK, :RANK] + corr[RANK:, RANK:]) + (corr[:RANK, RANK:] + corr[RANK:, :RANK])
        squares = jnp.where(diagonal, corr, 0.0)
        across = lax.rsqrt(jnp.sum(squares, axis=0, keepdims=True))
        down = lax.rsqrt(jnp.sum(squares, axis=1, keepdims=True))
        least = inverse_factor(corr * across * down, inv_ref)
        high, low = split_two(inv_ref[...] * across)
        weights = jnp.concatenate(
            [jnp.concatenate([high, high], axis=1), jnp.concatenate([low, jnp.zeros_like(low)], axis=1)], axis=0
        )
        for r in range(4):
            rows = pl.ds(r * 256, 256)
            both = dot_nt(pair_ref[side, rows, :], weights)
            value = both[:, :RANK] + both[:, RANK:]
            image_ref[rows, :] = value
            set_pair(0, rows, value)
        return least

    def step(carry):
        i, stop = carry

        @pl.when(i == 0)
        def _():
            start()
            for n in range(ITERS):
                multiply(n % 2)

        @pl.when(i > 0)
        def _():
            pl.when(i == 1)(start)
            multiply(0)

        least = orthonormalise(jnp.where(i == 0, ITERS % 2, 1))
        sound = least >= LEAST_PIVOT
        return i + 1, jnp.where(jnp.logical_and(i == 0, jnp.logical_not(sound)), ITERS + 1, stop)

    lax.while_loop(lambda carry: carry[0] < carry[1], step, (jnp.int32(0), jnp.int32(1)))

    own_rows = ROWS // SPLIT
    basis_ref[...] = image_ref[pl.ds(pl.multiple_of(lax.rem(mode * own_rows + core * 512, ROWS), own_rows), own_rows), :]
    total = jnp.zeros((RANK, field_ref.shape[1]), jnp.float32)
    for half in range(2):
        offset = pl.multiple_of(lax.rem(core * 512 + half * 512, ROWS), 512)
        total = total + dot_tn(pair_ref[0, pl.ds(half * 512, 512), :RANK], field_ref[pl.ds(offset, 512), :])
    core_ref[...] = total.reshape(core_ref.shape)


def on_device(unfolded, initial):
    held, cols = unfolded.shape[0], unfolded.shape[1] // SPLIT
    core, mode = lax.axis_index("core"), lax.axis_index(MODE)
    place = jnp.stack([core, mode, 2 * lax.axis_index("z0") + core]).astype(jnp.int32)
    vmem = pl.BlockSpec(memory_space=pltpu.VMEM)
    smem = pl.BlockSpec(memory_space=pltpu.SMEM)
    swap = [(0, 1), (1, 0)]

    parts = unfolded.reshape(held, SPLIT, cols).transpose(1, 0, 2)
    own = lax.all_to_all(parts, MODE, split_axis=0, concat_axis=0, tiled=True).reshape(ROWS, cols)
    twin = lax.ppermute(own, "core", swap)
    partial_gram, share = pl.pallas_call(
        gram_kernel,
        out_shape=(
            jax.ShapeDtypeStruct((SPLIT, 2, PAIR + 1, SLIVER, BLOCK), jnp.float32),
            jax.ShapeDtypeStruct((SHARE // SLIVER, SLIVER, RANK), jnp.float32),
        ),
        in_specs=[smem, vmem, vmem, vmem],
        out_specs=(vmem, vmem),
        compiler_params=pltpu.CompilerParams(vmem_limit_bytes=16 * 1024 * 1024),
        name="gram",
    )(place, own, twin, initial)

    partial_gram = partial_gram.astype(jnp.float16).reshape(2 * SPLIT, (PAIR + 1) * SLIVER, BLOCK)
    got = lax.all_to_all(partial_gram, PLANES, split_axis=0, concat_axis=0, tiled=True)
    got = got.astype(jnp.float32).reshape(2 * SPLIT, PAIR + 1, SLIVER, BLOCK)
    sliver = jnp.sum(got[:, :PAIR] * jnp.exp2(got[:, PAIR:] - HALF_TOP), axis=0)
    for axis in ("z1", "zh"):
        sliver = jnp.sum(lax.all_gather(sliver, axis, axis=0, tiled=False), axis=0)
    sliver = jnp.concatenate([sliver, share], axis=0)
    got = jnp.broadcast_to(sliver[None], (2 * SPLIT,) + sliver.shape)
    own_gram = lax.all_to_all(got, PLANES, split_axis=0, concat_axis=0, tiled=True)
    own_gram = own_gram.reshape((SPLIT, 2) + sliver.shape)
    twin_gram = lax.ppermute(own_gram, "core", swap)

    basis, core_rows = pl.pallas_call(
        iterate_kernel,
        out_shape=(
            jax.ShapeDtypeStruct((held, RANK), jnp.float32),
            jax.ShapeDtypeStruct((SPLIT, RANK // SPLIT, cols), jnp.float32),
        ),
        in_specs=[smem, vmem, vmem, vmem],
        out_specs=(vmem, vmem),
        scratch_shapes=[
            pltpu.VMEM((ROWS, ROWS), jnp.bfloat16),
            pltpu.VMEM((ROWS, ROWS), jnp.bfloat16),
            pltpu.VMEM((2, ROWS, 2 * RANK), jnp.bfloat16),
            pltpu.VMEM((ROWS, RANK), jnp.float32),
            pltpu.VMEM((RANK, RANK), jnp.float32),
        ],
        compiler_params=pltpu.CompilerParams(vmem_limit_bytes=32 * 1024 * 1024),
        name="iterate",
    )(place, own_gram, twin_gram, own)
    core_cols = lax.all_to_all(core_rows, MODE, split_axis=0, concat_axis=0, tiled=True)
    return basis, core_cols.transpose(1, 0, 2).reshape(RANK // SPLIT, SPLIT * cols)


def solution(mesh):
    chips = Mesh(mesh.devices.reshape(4, 4, mesh.devices.shape[1] // 8, 2, 2, 2), ("y", "x", "zh", "z1", "z0", "core"))
    rest = ("zh", "z1", "z0", "core")
    in_specs = (P(MODE, rest), P(MODE, None))
    out_specs = (P(MODE, None), P(MODE, rest))
    return jax.shard_map(on_device, mesh=chips, in_specs=in_specs, out_specs=out_specs, check_vma=False)
```

```python
import jax
import jax.numpy as jnp
from jax import lax
from jax.experimental import pallas as pl
from jax.experimental.pallas import tpu as pltpu
from jax.sharding import Mesh, PartitionSpec as P

ITERS = 4
ROWS = 1024
RANK = 128
BLOCK = 128
HALF_BLOCKS = 18
SPLIT = 16
SLIVER = BLOCK // SPLIT
LEAST_PIVOT = 5e-3
CHUNK = 256
MODE = ("y", "x")
PLANES = ("z0", "y", "x")
PAIR = HALF_BLOCKS // 2
SHARE = ROWS // SPLIT // 4
HALF_TOP = 14.0

SLOTS = [(t, t + d) for t in range(4) for d in range(4)]


def split_two(value):
    high = value.astype(jnp.bfloat16)
    return high, (value - high.astype(jnp.float32)).astype(jnp.bfloat16)


def dot_nt(left, right):
    return lax.dot_general(left, right, (((1,), (1,)), ((), ())), preferred_element_type=jnp.float32)


def dot_tn(left, right):
    return lax.dot_general(left, right, (((0,), (0,)), ((), ())), preferred_element_type=jnp.float32)


def dot_nn(left, right):
    return jnp.dot(left, right, preferred_element_type=jnp.float32)


def gram_kernel(place_ref, own_ref, twin_ref, initial_ref, out_ref, share_ref):
    core, quarter = place_ref[0], place_ref[2]
    rows_sent = pl.ds(pl.multiple_of(quarter * SHARE, SHARE), SHARE)
    share_ref[...] = initial_ref[rows_sent, :].reshape(share_ref.shape)

    def rows(ref, a):
        start = pl.multiple_of(lax.rem(core * 512 + a * 256, ROWS), 256)
        return ref[pl.ds(start, 256), :]

    own = [rows(own_ref, a) for a in range(4)]
    twin = [rows(twin_ref, a) for a in range(4)]
    tiles = {}
    for a, b in ((0, 0), (0, 1), (0, 2), (1, 1), (1, 2), (1, 3)):
        tiles[a, b] = dot_nt(own[a], own[b]) + dot_nt(twin[a], twin[b])

    def block(a, b):
        tile = tiles[a // 2, b // 2]
        return tile[(a % 2) * BLOCK : (a % 2 + 1) * BLOCK, (b % 2) * BLOCK : (b % 2 + 1) * BLOCK]

    blocks = [block(a, b) for a, b in SLOTS]
    blocks += [jnp.where(core == 0, block(s, s + 4), block(s + 2, s + 6)) for s in range(2)]
    largest = jnp.abs(blocks[0])
    for value in blocks[1:]:
        largest = jnp.maximum(largest, jnp.abs(value))
    largest = jnp.maximum(jnp.max(largest, axis=(0, 1), keepdims=True), 1e-30)
    power = jnp.round(jnp.log2(largest))
    scale = jnp.exp2(HALF_TOP - power)
    for slot, value in enumerate(blocks):
        value = (value * scale).reshape(SPLIT, SLIVER, BLOCK)
        out_ref[slot // PAIR, :, slot % PAIR] = value.astype(out_ref.dtype)
    power = jnp.broadcast_to(power, (SPLIT, SLIVER, BLOCK))
    for plane in range(2):
        out_ref[plane, :, PAIR] = power.astype(out_ref.dtype)


def inverse_factor(corr, inv_ref):
    panels = RANK // 8
    row = lax.broadcasted_iota(jnp.int32, (8, RANK), 0)
    lane = lax.broadcasted_iota(jnp.int32, (8, RANK), 1)
    rows = [corr[8 * p : 8 * p + 8, :] for p in range(panels)]
    least = jnp.full((8, RANK), jnp.inf, jnp.float32)

    def columns_of(value, p):
        return [jnp.broadcast_to(value[:, 8 * p + k : 8 * p + k + 1], (8, RANK)) for k in range(8)]

    for p in range(panels):
        inside = jnp.logical_and(lane >= 8 * p, lane < 8 * p + 8)
        column = columns_of(rows[p], p)
        here = jnp.where(inside, jnp.where(lane == row + 8 * p, 1.0, 0.0), rows[p])
        pivots = jnp.zeros((8, RANK), jnp.float32)
        steps = []
        for k in range(0, 8, 2):
            first, second = column[k], column[k + 1]
            a, b, c = first[k : k + 1], first[k + 1 : k + 2], second[k + 1 : k + 2]
            det = a * c - b * b
            inv_a, inv_det = 1.0 / a, 1.0 / det
            ratio, inv_c = b * inv_a, a * inv_det
            pivots = jnp.where(row == k, a, jnp.where(row == k + 1, det * inv_a, pivots))
            lower = jnp.where(row > k, first, 0.0)
            lowest = jnp.where(row > k + 1, second - first * ratio, 0.0)

            def heads(value):
                one = value[k : k + 1]
                two = (value[k + 1 : k + 2] - ratio * one) * inv_c
                return one * inv_a, two

            tops = [heads(column[later]) for later in range(k + 2, 8)]
            for later, (one, two) in zip(range(k + 2, 8), tops):
                column[later] = column[later] - lower * one - lowest * two
            side = heads(here)
            here = here - lower * side[0] - lowest * side[1]
            steps.append((k, ratio, tops, side))
        least = jnp.minimum(least, pivots)
        inv_ref[8 * p : 8 * p + 8, :] = jnp.where(lane < 8 * p + 8, here * lax.rsqrt(pivots), 0.0)
        for q in range(p + 1, panels):
            column = columns_of(rows[q], p)
            value = jnp.where(inside, 0.0, rows[q])
            for k, ratio, tops, side in steps:
                lower = column[k]
                lowest = column[k + 1] - lower * ratio
                for later, (one, two) in zip(range(k + 2, 8), tops):
                    column[later] = column[later] - lower * one - lowest * two
                value = value - lower * side[0] - lowest * side[1]
            rows[q] = value
    return jnp.min(least)


def iterate_kernel(place_ref, own_ref, twin_ref, field_ref, basis_ref, core_ref,
                   high_ref, low_ref, pair_ref, image_ref, inv_ref):
    core, mode = place_ref[0], place_ref[1]
    row = lax.broadcasted_iota(jnp.int32, (RANK, RANK), 0)
    diagonal = row == lax.broadcasted_iota(jnp.int32, (RANK, RANK), 1)
    largest = jnp.zeros((BLOCK, BLOCK), jnp.float32)

    def at(index):
        return pl.ds(index * BLOCK if isinstance(index, int) else pl.multiple_of(index * BLOCK, BLOCK), BLOCK)

    def put(a, b, value):
        high, low = split_two(value)
        high_ref[at(a), at(b)] = high
        low_ref[at(a), at(b)] = low
        if not (isinstance(a, int) and a == b):
            high, low = split_two(value.T)
            high_ref[at(b), at(a)] = high
            low_ref[at(b), at(a)] = low

    for slot, (a, b) in enumerate(SLOTS):
        for ref, shift in ((own_ref, 0), (twin_ref, 4)):
            value = ref[slot // PAIR, :, slot % PAIR].reshape(BLOCK, BLOCK)
            if a == b:
                largest = jnp.maximum(largest, jnp.where(diagonal, value, 0.0))
            put((a + shift) % 8, (b + shift) % 8, value)
    for s in range(2):
        put(2 * core + s, 2 * core + s + 4, own_ref[1, :, PAIR - 2 + s].reshape(BLOCK, BLOCK))
        put(6 - 2 * core + s, 2 - 2 * core + s, twin_ref[1, :, PAIR - 2 + s].reshape(BLOCK, BLOCK))
    scale = 1.0 / jnp.max(largest)

    def set_pair(side, rows, value):
        high, low = split_two(value)
        pair_ref[side, rows, :RANK] = high
        pair_ref[side, rows, RANK:] = low

    def start():
        for m in range(SPLIT):
            for plane in range(2):
                for ref, part in ((own_ref, core), (twin_ref, 1 - core)):
                    begin = m * (ROWS // SPLIT) + plane * 2 * SHARE + part * SHARE - core * 512 + ROWS
                    rows = pl.ds(pl.multiple_of(lax.rem(begin, ROWS), SHARE), SHARE)
                    set_pair(0, rows, ref[plane, m, PAIR:].reshape(SHARE, RANK))

    def multiply(side):
        for r in range(ROWS // CHUNK):
            rows = pl.ds(r * CHUNK, CHUNK)
            both = dot_nn(high_ref[rows, :], pair_ref[side])
            small = dot_nn(low_ref[rows, :], pair_ref[side, :, :RANK])
            set_pair(1 - side, rows, (both[:, :RANK] + (both[:, RANK:] + small)) * scale)

    def orthonormalise(side):
        corr = dot_tn(pair_ref[side], pair_ref[side])
        corr = (corr[:RANK, :RANK] + corr[RANK:, RANK:]) + (corr[:RANK, RANK:] + corr[RANK:, :RANK])
        squares = jnp.where(diagonal, corr, 0.0)
        across = lax.rsqrt(jnp.sum(squares, axis=0, keepdims=True))
        down = lax.rsqrt(jnp.sum(squares, axis=1, keepdims=True))
        least = inverse_factor(corr * across * down, inv_ref)
        high, low = split_two(inv_ref[...] * across)
        weights = jnp.concatenate(
            [jnp.concatenate([high, high], axis=1), jnp.concatenate([low, jnp.zeros_like(low)], axis=1)], axis=0
        )
        for r in range(4):
            rows = pl.ds(r * 256, 256)
            both = dot_nt(pair_ref[side, rows, :], weights)
            value = both[:, :RANK] + both[:, RANK:]
            image_ref[rows, :] = value
            set_pair(0, rows, value)
        return least

    def step(carry):
        i, stop = carry

        @pl.when(i == 0)
        def _():
            start()
            for n in range(ITERS):
                multiply(n % 2)

        @pl.when(i > 0)
        def _():
            pl.when(i == 1)(start)
            multiply(0)

        least = orthonormalise(jnp.where(i == 0, ITERS % 2, 1))
        sound = least >= LEAST_PIVOT
        return i + 1, jnp.where(jnp.logical_and(i == 0, jnp.logical_not(sound)), ITERS + 1, stop)

    lax.while_loop(lambda carry: carry[0] < carry[1], step, (jnp.int32(0), jnp.int32(1)))

    own_rows = ROWS // SPLIT
    basis_ref[...] = image_ref[pl.ds(pl.multiple_of(lax.rem(mode * own_rows + core * 512, ROWS), own_rows), own_rows), :]
    total = jnp.zeros((RANK, field_ref.shape[1]), jnp.float32)
    for half in range(2):
        offset = pl.multiple_of(lax.rem(core * 512 + half * 512, ROWS), 512)
        total = total + dot_tn(pair_ref[0, pl.ds(half * 512, 512), :RANK], field_ref[pl.ds(offset, 512), :])
    core_ref[...] = total.reshape(core_ref.shape)


def on_device(unfolded, initial):
    held, cols = unfolded.shape[0], unfolded.shape[1] // SPLIT
    core, mode = lax.axis_index("core"), lax.axis_index(MODE)
    place = jnp.stack([core, mode, 2 * lax.axis_index("z0") + core]).astype(jnp.int32)
    vmem = pl.BlockSpec(memory_space=pltpu.VMEM)
    smem = pl.BlockSpec(memory_space=pltpu.SMEM)
    swap = [(0, 1), (1, 0)]

    parts = unfolded.reshape(held, SPLIT, cols).transpose(1, 0, 2)
    own = lax.all_to_all(parts, MODE, split_axis=0, concat_axis=0, tiled=True).reshape(ROWS, cols)
    twin = lax.ppermute(own, "core", swap)
    partial_gram, share = pl.pallas_call(
        gram_kernel,
        out_shape=(
            jax.ShapeDtypeStruct((2, SPLIT, PAIR + 1, SLIVER, BLOCK), jnp.float32),
            jax.ShapeDtypeStruct((SHARE // SLIVER, SLIVER, RANK), jnp.float32),
        ),
        in_specs=[smem, vmem, vmem, vmem],
        out_specs=(vmem, vmem),
        compiler_params=pltpu.CompilerParams(vmem_limit_bytes=16 * 1024 * 1024),
        name="gram",
    )(place, own, twin, initial)

    partial_gram = partial_gram.astype(jnp.float16).reshape(2 * SPLIT, (PAIR + 1) * SLIVER, BLOCK)
    got = lax.all_to_all(partial_gram, PLANES, split_axis=0, concat_axis=0, tiled=True)
    got = got.astype(jnp.float32).reshape(2 * SPLIT, PAIR + 1, SLIVER, BLOCK)
    sliver = jnp.sum(got[:, :PAIR] * jnp.exp2(got[:, PAIR:] - HALF_TOP), axis=0)
    for axis in ("z1", "zh"):
        sliver = jnp.sum(lax.all_gather(sliver, axis, axis=0, tiled=False), axis=0)
    sliver = jnp.concatenate([sliver, share], axis=0)
    got = jnp.broadcast_to(sliver[None], (2 * SPLIT,) + sliver.shape)
    own_gram = lax.all_to_all(got, PLANES, split_axis=0, concat_axis=0, tiled=True)
    own_gram = own_gram.reshape((2, SPLIT) + sliver.shape)
    twin_gram = lax.ppermute(own_gram, "core", swap)

    basis, core_rows = pl.pallas_call(
        iterate_kernel,
        out_shape=(
            jax.ShapeDtypeStruct((held, RANK), jnp.float32),
            jax.ShapeDtypeStruct((SPLIT, RANK // SPLIT, cols), jnp.float32),
        ),
        in_specs=[smem, vmem, vmem, vmem],
        out_specs=(vmem, vmem),
        scratch_shapes=[
            pltpu.VMEM((ROWS, ROWS), jnp.bfloat16),
            pltpu.VMEM((ROWS, ROWS), jnp.bfloat16),
            pltpu.VMEM((2, ROWS, 2 * RANK), jnp.bfloat16),
            pltpu.VMEM((ROWS, RANK), jnp.float32),
            pltpu.VMEM((RANK, RANK), jnp.float32),
        ],
        compiler_params=pltpu.CompilerParams(vmem_limit_bytes=32 * 1024 * 1024),
        name="iterate",
    )(place, own_gram, twin_gram, own)
    core_cols = lax.all_to_all(core_rows, MODE, split_axis=0, concat_axis=0, tiled=True)
    return basis, core_cols.transpose(1, 0, 2).reshape(RANK // SPLIT, SPLIT * cols)


def solution(mesh):
    chips = Mesh(mesh.devices.reshape(4, 4, mesh.devices.shape[1] // 8, 2, 2, 2), ("y", "x", "zh", "z1", "z0", "core"))
    rest = ("zh", "z1", "z0", "core")
    in_specs = (P(MODE, rest), P(MODE, None))
    out_specs = (P(MODE, None), P(MODE, rest))
    return jax.shard_map(on_device, mesh=chips, in_specs=in_specs, out_specs=out_specs, check_vma=False)
```

```python
import jax
import jax.numpy as jnp
from jax import lax
from jax.experimental import pallas as pl
from jax.experimental.pallas import tpu as pltpu
from jax.sharding import Mesh, PartitionSpec as P

ITERS = 4
ROWS = 1024
RANK = 128
BLOCK = 128
HALF_BLOCKS = 18
SPLIT = 16
SLIVER = BLOCK // SPLIT
LEAST_PIVOT = 5e-3
CHUNK = 256
MODE = ("x", "y")
PLANES = ("z0", "x", "y")
PAIR = HALF_BLOCKS // 2
SHARE = ROWS // SPLIT // 4
HALF_TOP = 14.0

SLOTS = [(t, t + d) for t in range(4) for d in range(4)]


def split_two(value):
    high = value.astype(jnp.bfloat16)
    return high, (value - high.astype(jnp.float32)).astype(jnp.bfloat16)


def dot_nt(left, right):
    return lax.dot_general(left, right, (((1,), (1,)), ((), ())), preferred_element_type=jnp.float32)


def dot_tn(left, right):
    return lax.dot_general(left, right, (((0,), (0,)), ((), ())), preferred_element_type=jnp.float32)


def dot_nn(left, right):
    return jnp.dot(left, right, preferred_element_type=jnp.float32)


def gram_kernel(place_ref, own_ref, twin_ref, initial_ref, out_ref, share_ref):
    core, quarter = place_ref[0], place_ref[2]
    rows_sent = pl.ds(pl.multiple_of(quarter * SHARE, SHARE), SHARE)
    share_ref[...] = initial_ref[rows_sent, :].reshape(share_ref.shape)

    def rows(ref, a):
        start = pl.multiple_of(lax.rem(core * 512 + a * 256, ROWS), 256)
        return ref[pl.ds(start, 256), :]

    own = [rows(own_ref, a) for a in range(4)]
    twin = [rows(twin_ref, a) for a in range(4)]
    tiles = {}
    for a, b in ((0, 0), (0, 1), (0, 2), (1, 1), (1, 2), (1, 3)):
        tiles[a, b] = dot_nt(own[a], own[b]) + dot_nt(twin[a], twin[b])

    def block(a, b):
        tile = tiles[a // 2, b // 2]
        return tile[(a % 2) * BLOCK : (a % 2 + 1) * BLOCK, (b % 2) * BLOCK : (b % 2 + 1) * BLOCK]

    blocks = [block(a, b) for a, b in SLOTS]
    blocks += [jnp.where(core == 0, block(s, s + 4), block(s + 2, s + 6)) for s in range(2)]
    largest = jnp.abs(blocks[0])
    for value in blocks[1:]:
        largest = jnp.maximum(largest, jnp.abs(value))
    largest = jnp.maximum(jnp.max(largest, axis=(0, 1), keepdims=True), 1e-30)
    power = jnp.round(jnp.log2(largest))
    scale = jnp.exp2(HALF_TOP - power)
    for slot, value in enumerate(blocks):
        value = (value * scale).reshape(SPLIT, SLIVER, BLOCK)
        out_ref[slot // PAIR, :, slot % PAIR] = value.astype(out_ref.dtype)
    power = jnp.broadcast_to(power, (SPLIT, SLIVER, BLOCK))
    for plane in range(2):
        out_ref[plane, :, PAIR] = power.astype(out_ref.dtype)


def inverse_factor(corr, inv_ref):
    panels = RANK // 8
    row = lax.broadcasted_iota(jnp.int32, (8, RANK), 0)
    lane = lax.broadcasted_iota(jnp.int32, (8, RANK), 1)
    rows = [corr[8 * p : 8 * p + 8, :] for p in range(panels)]
    least = jnp.full((8, RANK), jnp.inf, jnp.float32)

    def columns_of(value, p):
        return [jnp.broadcast_to(value[:, 8 * p + k : 8 * p + k + 1], (8, RANK)) for k in range(8)]

    for p in range(panels):
        inside = jnp.logical_and(lane >= 8 * p, lane < 8 * p + 8)
        column = columns_of(rows[p], p)
        here = jnp.where(inside, jnp.where(lane == row + 8 * p, 1.0, 0.0), rows[p])
        pivots = jnp.zeros((8, RANK), jnp.float32)
        steps = []
        for k in range(0, 8, 2):
            first, second = column[k], column[k + 1]
            a, b, c = first[k : k + 1], first[k + 1 : k + 2], second[k + 1 : k + 2]
            det = a * c - b * b
            inv_a, inv_det = 1.0 / a, 1.0 / det
            ratio, inv_c = b * inv_a, a * inv_det
            pivots = jnp.where(row == k, a, jnp.where(row == k + 1, det * inv_a, pivots))
            lower = jnp.where(row > k, first, 0.0)
            lowest = jnp.where(row > k + 1, second - first * ratio, 0.0)

            def heads(value):
                one = value[k : k + 1]
                two = (value[k + 1 : k + 2] - ratio * one) * inv_c
                return one * inv_a, two

            tops = [heads(column[later]) for later in range(k + 2, 8)]
            for later, (one, two) in zip(range(k + 2, 8), tops):
                column[later] = column[later] - lower * one - lowest * two
            side = heads(here)
            here = here - lower * side[0] - lowest * side[1]
            steps.append((k, ratio, tops, side))
        least = jnp.minimum(least, pivots)
        inv_ref[8 * p : 8 * p + 8, :] = jnp.where(lane < 8 * p + 8, here * lax.rsqrt(pivots), 0.0)
        for q in range(p + 1, panels):
            column = columns_of(rows[q], p)
            value = jnp.where(inside, 0.0, rows[q])
            for k, ratio, tops, side in steps:
                lower = column[k]
                lowest = column[k + 1] - lower * ratio
                for later, (one, two) in zip(range(k + 2, 8), tops):
                    column[later] = column[later] - lower * one - lowest * two
                value = value - lower * side[0] - lowest * side[1]
            rows[q] = value
    return jnp.min(least)


def iterate_kernel(place_ref, own_ref, twin_ref, field_ref, basis_ref, core_ref,
                   high_ref, low_ref, pair_ref, image_ref, inv_ref):
    core, mode = place_ref[0], place_ref[1]
    row = lax.broadcasted_iota(jnp.int32, (RANK, RANK), 0)
    diagonal = row == lax.broadcasted_iota(jnp.int32, (RANK, RANK), 1)
    largest = jnp.zeros((BLOCK, BLOCK), jnp.float32)

    def at(index):
        return pl.ds(index * BLOCK if isinstance(index, int) else pl.multiple_of(index * BLOCK, BLOCK), BLOCK)

    def put(a, b, value):
        high, low = split_two(value)
        high_ref[at(a), at(b)] = high
        low_ref[at(a), at(b)] = low
        if not (isinstance(a, int) and a == b):
            high, low = split_two(value.T)
            high_ref[at(b), at(a)] = high
            low_ref[at(b), at(a)] = low

    for slot, (a, b) in enumerate(SLOTS):
        for ref, shift in ((own_ref, 0), (twin_ref, 4)):
            value = ref[slot // PAIR, :, slot % PAIR].reshape(BLOCK, BLOCK)
            if a == b:
                largest = jnp.maximum(largest, jnp.where(diagonal, value, 0.0))
            put((a + shift) % 8, (b + shift) % 8, value)
    for s in range(2):
        put(2 * core + s, 2 * core + s + 4, own_ref[1, :, PAIR - 2 + s].reshape(BLOCK, BLOCK))
        put(6 - 2 * core + s, 2 - 2 * core + s, twin_ref[1, :, PAIR - 2 + s].reshape(BLOCK, BLOCK))
    scale = 1.0 / jnp.max(largest)

    def set_pair(side, rows, value):
        high, low = split_two(value)
        pair_ref[side, rows, :RANK] = high
        pair_ref[side, rows, RANK:] = low

    def start():
        for m in range(SPLIT):
            for plane in range(2):
                for ref, part in ((own_ref, core), (twin_ref, 1 - core)):
                    begin = m * (ROWS // SPLIT) + plane * 2 * SHARE + part * SHARE - core * 512 + ROWS
                    rows = pl.ds(pl.multiple_of(lax.rem(begin, ROWS), SHARE), SHARE)
                    set_pair(0, rows, ref[plane, m, PAIR:].reshape(SHARE, RANK))

    def multiply(side):
        for r in range(ROWS // CHUNK):
            rows = pl.ds(r * CHUNK, CHUNK)
            both = dot_nn(high_ref[rows, :], pair_ref[side])
            small = dot_nn(low_ref[rows, :], pair_ref[side, :, :RANK])
            set_pair(1 - side, rows, (both[:, :RANK] + (both[:, RANK:] + small)) * scale)

    def orthonormalise(side):
        corr = dot_tn(pair_ref[side], pair_ref[side])
        corr = (corr[:RANK, :RANK] + corr[RANK:, RANK:]) + (corr[:RANK, RANK:] + corr[RANK:, :RANK])
        squares = jnp.where(diagonal, corr, 0.0)
        across = lax.rsqrt(jnp.sum(squares, axis=0, keepdims=True))
        down = lax.rsqrt(jnp.sum(squares, axis=1, keepdims=True))
        least = inverse_factor(corr * across * down, inv_ref)
        high, low = split_two(inv_ref[...] * across)
        weights = jnp.concatenate(
            [jnp.concatenate([high, high], axis=1), jnp.concatenate([low, jnp.zeros_like(low)], axis=1)], axis=0
        )
        for r in range(4):
            rows = pl.ds(r * 256, 256)
            both = dot_nt(pair_ref[side, rows, :], weights)
            value = both[:, :RANK] + both[:, RANK:]
            image_ref[rows, :] = value
            set_pair(0, rows, value)
        return least

    def step(carry):
        i, stop = carry

        @pl.when(i == 0)
        def _():
            start()
            for n in range(ITERS):
                multiply(n % 2)

        @pl.when(i > 0)
        def _():
            pl.when(i == 1)(start)
            multiply(0)

        least = orthonormalise(jnp.where(i == 0, ITERS % 2, 1))
        sound = least >= LEAST_PIVOT
        return i + 1, jnp.where(jnp.logical_and(i == 0, jnp.logical_not(sound)), ITERS + 1, stop)

    lax.while_loop(lambda carry: carry[0] < carry[1], step, (jnp.int32(0), jnp.int32(1)))

    own_rows = ROWS // SPLIT
    basis_ref[...] = image_ref[pl.ds(pl.multiple_of(lax.rem(mode * own_rows + core * 512, ROWS), own_rows), own_rows), :]
    total = jnp.zeros((RANK, field_ref.shape[1]), jnp.float32)
    for half in range(2):
        offset = pl.multiple_of(lax.rem(core * 512 + half * 512, ROWS), 512)
        total = total + dot_tn(pair_ref[0, pl.ds(half * 512, 512), :RANK], field_ref[pl.ds(offset, 512), :])
    total = total.reshape(core_ref.shape)
    for x in range(4):
        for y in range(4):
            core_ref[4 * x + y] = total[4 * y + x]


def on_device(unfolded, initial):
    held, cols = unfolded.shape[0], unfolded.shape[1] // SPLIT
    core, mode = lax.axis_index("core"), lax.axis_index(MODE)
    place = jnp.stack([core, mode, 2 * lax.axis_index("z0") + core]).astype(jnp.int32)
    vmem = pl.BlockSpec(memory_space=pltpu.VMEM)
    smem = pl.BlockSpec(memory_space=pltpu.SMEM)
    swap = [(0, 1), (1, 0)]

    parts = unfolded.reshape(held, SPLIT, cols).transpose(1, 0, 2)
    own = lax.all_to_all(parts, MODE, split_axis=0, concat_axis=0, tiled=True).reshape(ROWS, cols)
    twin = lax.ppermute(own, "core", swap)
    partial_gram, share = pl.pallas_call(
        gram_kernel,
        out_shape=(
            jax.ShapeDtypeStruct((2, SPLIT, PAIR + 1, SLIVER, BLOCK), jnp.float32),
            jax.ShapeDtypeStruct((SHARE // SLIVER, SLIVER, RANK), jnp.float32),
        ),
        in_specs=[smem, vmem, vmem, vmem],
        out_specs=(vmem, vmem),
        compiler_params=pltpu.CompilerParams(vmem_limit_bytes=16 * 1024 * 1024),
        name="gram",
    )(place, own, twin, initial)

    partial_gram = partial_gram.astype(jnp.float16).reshape(2 * SPLIT, (PAIR + 1) * SLIVER, BLOCK)
    got = lax.all_to_all(partial_gram, PLANES, split_axis=0, concat_axis=0, tiled=True)
    got = got.astype(jnp.float32).reshape(2 * SPLIT, PAIR + 1, SLIVER, BLOCK)
    sliver = jnp.sum(got[:, :PAIR] * jnp.exp2(got[:, PAIR:] - HALF_TOP), axis=0)
    for axis in ("z1", "zh"):
        sliver = jnp.sum(lax.all_gather(sliver, axis, axis=0, tiled=False), axis=0)
    sliver = jnp.concatenate([sliver, share], axis=0)
    got = jnp.broadcast_to(sliver[None], (2 * SPLIT,) + sliver.shape)
    own_gram = lax.all_to_all(got, PLANES, split_axis=0, concat_axis=0, tiled=True)
    own_gram = own_gram.reshape((2, SPLIT) + sliver.shape)
    twin_gram = lax.ppermute(own_gram, "core", swap)

    basis, core_rows = pl.pallas_call(
        iterate_kernel,
        out_shape=(
            jax.ShapeDtypeStruct((held, RANK), jnp.float32),
            jax.ShapeDtypeStruct((SPLIT, RANK // SPLIT, cols), jnp.float32),
        ),
        in_specs=[smem, vmem, vmem, vmem],
        out_specs=(vmem, vmem),
        scratch_shapes=[
            pltpu.VMEM((ROWS, ROWS), jnp.bfloat16),
            pltpu.VMEM((ROWS, ROWS), jnp.bfloat16),
            pltpu.VMEM((2, ROWS, 2 * RANK), jnp.bfloat16),
            pltpu.VMEM((ROWS, RANK), jnp.float32),
            pltpu.VMEM((RANK, RANK), jnp.float32),
        ],
        compiler_params=pltpu.CompilerParams(vmem_limit_bytes=32 * 1024 * 1024),
        name="iterate",
    )(place, own_gram, twin_gram, own)
    core_cols = lax.all_to_all(core_rows, MODE, split_axis=0, concat_axis=0, tiled=True)
    return basis, core_cols.transpose(1, 0, 2).reshape(RANK // SPLIT, SPLIT * cols)


def solution(mesh):
    chips = Mesh(mesh.devices.reshape(4, 4, mesh.devices.shape[1] // 8, 2, 2, 2), ("y", "x", "zh", "z1", "z0", "core"))
    mode = ("y", "x")
    rest = ("zh", "z1", "z0", "core")
    in_specs = (P(mode, rest), P(mode, None))
    out_specs = (P(mode, None), P(mode, rest))
    return jax.shard_map(on_device, mesh=chips, in_specs=in_specs, out_specs=out_specs, check_vma=False)
```

```python
import jax
import jax.numpy as jnp
from jax import lax
from jax.experimental import pallas as pl
from jax.experimental.pallas import tpu as pltpu
from jax.sharding import Mesh, PartitionSpec as P

ITERS = 4
ROWS = 1024
RANK = 128
BLOCK = 128
HALF_BLOCKS = 18
SPLIT = 16
SLIVER = BLOCK // SPLIT
LEAST_PIVOT = 5e-3
CHUNK = 256
MODE = ("x", "y")
PLANES = ("z0", "x", "y")
PAIR = HALF_BLOCKS // 2
SHARE = ROWS // SPLIT // 4
HALF_TOP = 14.0

SLOTS = [(t, t + d) for t in range(4) for d in range(4)]


def split_two(value):
    high = value.astype(jnp.bfloat16)
    return high, (value - high.astype(jnp.float32)).astype(jnp.bfloat16)


def dot_nt(left, right):
    return lax.dot_general(left, right, (((1,), (1,)), ((), ())), preferred_element_type=jnp.float32)


def dot_tn(left, right):
    return lax.dot_general(left, right, (((0,), (0,)), ((), ())), preferred_element_type=jnp.float32)


def dot_nn(left, right):
    return jnp.dot(left, right, preferred_element_type=jnp.float32)


def gram_kernel(place_ref, own_ref, twin_ref, initial_ref, out_ref, share_ref):
    core, quarter = place_ref[0], place_ref[2]
    rows_sent = pl.ds(pl.multiple_of(quarter * SHARE, SHARE), SHARE)
    share_ref[...] = initial_ref[rows_sent, :].reshape(share_ref.shape)

    def rows(ref, a):
        start = pl.multiple_of(lax.rem(core * 512 + a * 256, ROWS), 256)
        return ref[pl.ds(start, 256), :]

    own = [rows(own_ref, a) for a in range(4)]
    twin = [rows(twin_ref, a) for a in range(4)]
    tiles = {}
    for a, b in ((0, 0), (0, 1), (0, 2), (1, 1), (1, 2), (1, 3)):
        tiles[a, b] = dot_nt(own[a], own[b]) + dot_nt(twin[a], twin[b])

    def block(a, b):
        tile = tiles[a // 2, b // 2]
        return tile[(a % 2) * BLOCK : (a % 2 + 1) * BLOCK, (b % 2) * BLOCK : (b % 2 + 1) * BLOCK]

    blocks = [block(a, b) for a, b in SLOTS]
    blocks += [jnp.where(core == 0, block(s, s + 4), block(s + 2, s + 6)) for s in range(2)]
    largest = jnp.abs(blocks[0])
    for value in blocks[1:]:
        largest = jnp.maximum(largest, jnp.abs(value))
    largest = jnp.maximum(jnp.max(largest, axis=(0, 1), keepdims=True), 1e-30)
    power = jnp.round(jnp.log2(largest))
    scale = jnp.exp2(HALF_TOP - power)
    for slot, value in enumerate(blocks):
        value = (value * scale).reshape(SPLIT, SLIVER, BLOCK)
        out_ref[slot // PAIR, :, slot % PAIR] = value.astype(out_ref.dtype)
    power = jnp.broadcast_to(power, (SPLIT, SLIVER, BLOCK))
    for plane in range(2):
        out_ref[plane, :, PAIR] = power.astype(out_ref.dtype)


def inverse_factor(corr, inv_ref):
    panels = RANK // 8
    row = lax.broadcasted_iota(jnp.int32, (8, RANK), 0)
    lane = lax.broadcasted_iota(jnp.int32, (8, RANK), 1)
    rows = [corr[8 * p : 8 * p + 8, :] for p in range(panels)]
    least = jnp.full((8, RANK), jnp.inf, jnp.float32)

    def columns_of(value, p):
        return [jnp.broadcast_to(value[:, 8 * p + k : 8 * p + k + 1], (8, RANK)) for k in range(8)]

    for p in range(panels):
        inside = jnp.logical_and(lane >= 8 * p, lane < 8 * p + 8)
        column = columns_of(rows[p], p)
        here = jnp.where(inside, jnp.where(lane == row + 8 * p, 1.0, 0.0), rows[p])
        pivots = jnp.zeros((8, RANK), jnp.float32)
        steps = []
        for k in range(0, 8, 2):
            first, second = column[k], column[k + 1]
            a, b, c = first[k : k + 1], first[k + 1 : k + 2], second[k + 1 : k + 2]
            det = a * c - b * b
            inv_a, inv_det = 1.0 / a, 1.0 / det
            ratio, inv_c = b * inv_a, a * inv_det
            pivots = jnp.where(row == k, a, jnp.where(row == k + 1, det * inv_a, pivots))
            lower = jnp.where(row > k, first, 0.0)
            lowest = jnp.where(row > k + 1, second - first * ratio, 0.0)

            def heads(value):
                one = value[k : k + 1]
                two = (value[k + 1 : k + 2] - ratio * one) * inv_c
                return one * inv_a, two

            tops = [heads(column[later]) for later in range(k + 2, 8)]
            for later, (one, two) in zip(range(k + 2, 8), tops):
                column[later] = column[later] - lower * one - lowest * two
            side = heads(here)
            here = here - lower * side[0] - lowest * side[1]
            steps.append((k, ratio, tops, side))
        least = jnp.minimum(least, pivots)
        inv_ref[8 * p : 8 * p + 8, :] = jnp.where(lane < 8 * p + 8, here * lax.rsqrt(pivots), 0.0)
        for q in range(p + 1, panels):
            column = columns_of(rows[q], p)
            value = jnp.where(inside, 0.0, rows[q])
            for k, ratio, tops, side in steps:
                lower = column[k]
                lowest = column[k + 1] - lower * ratio
                for later, (one, two) in zip(range(k + 2, 8), tops):
                    column[later] = column[later] - lower * one - lowest * two
                value = value - lower * side[0] - lowest * side[1]
            rows[q] = value
    return jnp.min(least)


def iterate_kernel(place_ref, own_ref, twin_ref, field_ref, basis_ref, core_ref,
                   high_ref, low_ref, pair_ref, image_ref, inv_ref):
    core, mode = place_ref[0], place_ref[1]
    row = lax.broadcasted_iota(jnp.int32, (RANK, RANK), 0)
    diagonal = row == lax.broadcasted_iota(jnp.int32, (RANK, RANK), 1)
    largest = jnp.zeros((BLOCK, BLOCK), jnp.float32)

    def at(index):
        return pl.ds(index * BLOCK if isinstance(index, int) else pl.multiple_of(index * BLOCK, BLOCK), BLOCK)

    def put(a, b, value):
        high, low = split_two(value)
        high_ref[at(a), at(b)] = high
        low_ref[at(a), at(b)] = low
        if not (isinstance(a, int) and a == b):
            high, low = split_two(value.T)
            high_ref[at(b), at(a)] = high
            low_ref[at(b), at(a)] = low

    for slot, (a, b) in enumerate(SLOTS):
        for ref, shift in ((own_ref, 0), (twin_ref, 4)):
            value = ref[slot // PAIR, :, slot % PAIR].reshape(BLOCK, BLOCK)
            if a == b:
                largest = jnp.maximum(largest, jnp.where(diagonal, value, 0.0))
            put((a + shift) % 8, (b + shift) % 8, value)
    for s in range(2):
        put(2 * core + s, 2 * core + s + 4, own_ref[1, :, PAIR - 2 + s].reshape(BLOCK, BLOCK))
        put(6 - 2 * core + s, 2 - 2 * core + s, twin_ref[1, :, PAIR - 2 + s].reshape(BLOCK, BLOCK))
    scale = 1.0 / jnp.max(largest)

    def set_pair(side, rows, value):
        high, low = split_two(value)
        pair_ref[side, rows, :RANK] = high
        pair_ref[side, rows, RANK:] = low

    def start():
        for m in range(SPLIT):
            for plane in range(2):
                for ref, part in ((own_ref, core), (twin_ref, 1 - core)):
                    begin = m * (ROWS // SPLIT) + plane * 2 * SHARE + part * SHARE - core * 512 + ROWS
                    rows = pl.ds(pl.multiple_of(lax.rem(begin, ROWS), SHARE), SHARE)
                    set_pair(0, rows, ref[plane, m, PAIR:].reshape(SHARE, RANK))

    def multiply(side):
        for r in range(ROWS // CHUNK):
            rows = pl.ds(r * CHUNK, CHUNK)
            both = dot_nn(high_ref[rows, :], pair_ref[side])
            small = dot_nn(low_ref[rows, :], pair_ref[side, :, :RANK])
            set_pair(1 - side, rows, (both[:, :RANK] + (both[:, RANK:] + small)) * scale)

    def orthonormalise(side):
        corr = dot_tn(pair_ref[side], pair_ref[side])
        corr = (corr[:RANK, :RANK] + corr[RANK:, RANK:]) + (corr[:RANK, RANK:] + corr[RANK:, :RANK])
        squares = jnp.where(diagonal, corr, 0.0)
        across = lax.rsqrt(jnp.sum(squares, axis=0, keepdims=True))
        down = lax.rsqrt(jnp.sum(squares, axis=1, keepdims=True))
        least = inverse_factor(corr * across * down, inv_ref)
        high, low = split_two(inv_ref[...] * across)
        weights = jnp.concatenate(
            [jnp.concatenate([high, high], axis=1), jnp.concatenate([low, jnp.zeros_like(low)], axis=1)], axis=0
        )
        for r in range(4):
            rows = pl.ds(r * 256, 256)
            both = dot_nt(pair_ref[side, rows, :], weights)
            value = both[:, :RANK] + both[:, RANK:]
            image_ref[rows, :] = value
            set_pair(0, rows, value)
        return least

    def step(carry):
        i, stop = carry

        @pl.when(i == 0)
        def _():
            start()
            for n in range(ITERS):
                multiply(n % 2)

        @pl.when(i > 0)
        def _():
            pl.when(i == 1)(start)
            multiply(0)

        least = orthonormalise(jnp.where(i == 0, ITERS % 2, 1))
        sound = least >= LEAST_PIVOT
        return i + 1, jnp.where(jnp.logical_and(i == 0, jnp.logical_not(sound)), ITERS + 1, stop)

    lax.while_loop(lambda carry: carry[0] < carry[1], step, (jnp.int32(0), jnp.int32(1)))

    own_rows = ROWS // SPLIT
    basis_ref[...] = image_ref[pl.ds(pl.multiple_of(lax.rem(mode * own_rows + core * 512, ROWS), own_rows), own_rows), :]
    total = jnp.zeros((RANK, field_ref.shape[1]), jnp.float32)
    for half in range(2):
        offset = pl.multiple_of(lax.rem(core * 512 + half * 512, ROWS), 512)
        total = total + dot_tn(pair_ref[0, pl.ds(half * 512, 512), :RANK], field_ref[pl.ds(offset, 512), :])
    total = total.reshape(core_ref.shape)
    for x in range(4):
        for y in range(4):
            core_ref[4 * x + y] = total[4 * y + x]


def on_device(unfolded, initial):
    held, cols = unfolded.shape[0], unfolded.shape[1] // SPLIT
    core, mode = lax.axis_index("core"), lax.axis_index(MODE)
    place = jnp.stack([core, mode, 2 * lax.axis_index("z0") + core]).astype(jnp.int32)
    vmem = pl.BlockSpec(memory_space=pltpu.VMEM)
    smem = pl.BlockSpec(memory_space=pltpu.SMEM)
    swap = [(0, 1), (1, 0)]

    parts = unfolded.reshape(held, SPLIT, cols).transpose(1, 0, 2)
    own = lax.all_to_all(parts, MODE, split_axis=0, concat_axis=0, tiled=True).reshape(ROWS, cols)
    twin = lax.ppermute(own, "core", swap)
    partial_gram, share = pl.pallas_call(
        gram_kernel,
        out_shape=(
            jax.ShapeDtypeStruct((2, SPLIT, PAIR + 1, SLIVER, BLOCK), jnp.float32),
            jax.ShapeDtypeStruct((SHARE // SLIVER, SLIVER, RANK), jnp.float32),
        ),
        in_specs=[smem, vmem, vmem, vmem],
        out_specs=(vmem, vmem),
        compiler_params=pltpu.CompilerParams(vmem_limit_bytes=16 * 1024 * 1024),
        name="gram",
    )(place, own, twin, initial)

    partial_gram = partial_gram.astype(jnp.float16).reshape(2 * SPLIT, (PAIR + 1) * SLIVER, BLOCK)
    got = lax.all_to_all(partial_gram, PLANES, split_axis=0, concat_axis=0, tiled=True)
    got = got.astype(jnp.float32).reshape(2 * SPLIT, PAIR + 1, SLIVER, BLOCK)
    sliver = jnp.sum(got[:, :PAIR] * jnp.exp2(got[:, PAIR:] - HALF_TOP), axis=0)
    for axis in ("zh", "z1"):
        sliver = jnp.sum(lax.all_gather(sliver, axis, axis=0, tiled=False), axis=0)
    sliver = jnp.concatenate([sliver, share], axis=0)
    got = jnp.broadcast_to(sliver[None], (2 * SPLIT,) + sliver.shape)
    own_gram = lax.all_to_all(got, PLANES, split_axis=0, concat_axis=0, tiled=True)
    own_gram = own_gram.reshape((2, SPLIT) + sliver.shape)
    twin_gram = lax.ppermute(own_gram, "core", swap)

    basis, core_rows = pl.pallas_call(
        iterate_kernel,
        out_shape=(
            jax.ShapeDtypeStruct((held, RANK), jnp.float32),
            jax.ShapeDtypeStruct((SPLIT, RANK // SPLIT, cols), jnp.float32),
        ),
        in_specs=[smem, vmem, vmem, vmem],
        out_specs=(vmem, vmem),
        scratch_shapes=[
            pltpu.VMEM((ROWS, ROWS), jnp.bfloat16),
            pltpu.VMEM((ROWS, ROWS), jnp.bfloat16),
            pltpu.VMEM((2, ROWS, 2 * RANK), jnp.bfloat16),
            pltpu.VMEM((ROWS, RANK), jnp.float32),
            pltpu.VMEM((RANK, RANK), jnp.float32),
        ],
        compiler_params=pltpu.CompilerParams(vmem_limit_bytes=32 * 1024 * 1024),
        name="iterate",
    )(place, own_gram, twin_gram, own)
    core_cols = lax.all_to_all(core_rows, MODE, split_axis=0, concat_axis=0, tiled=True)
    return basis, core_cols.transpose(1, 0, 2).reshape(RANK // SPLIT, SPLIT * cols)


def solution(mesh):
    chips = Mesh(mesh.devices.reshape(4, 4, mesh.devices.shape[1] // 8, 2, 2, 2), ("y", "x", "zh", "z1", "z0", "core"))
    mode = ("y", "x")
    rest = ("zh", "z1", "z0", "core")
    in_specs = (P(mode, rest), P(mode, None))
    out_specs = (P(mode, None), P(mode, rest))
    return jax.shard_map(on_device, mesh=chips, in_specs=in_specs, out_specs=out_specs, check_vma=False)
```
